128 devices in a mesh: grp: 8 (over z, core), sub: 16 (over y, x).
Axes of the slice: x: 4, y: 4, z: 4, core: 2. Of those that a mesh axis runs over, the one named last changes fastest.
Arguments:
- potential: float32 [2048, 4096], P(('grp', 'sub')), may hold values from -6 to 6
- right_side: float32 [2048, 4096], P(('grp', 'sub')), may hold values from -6.5 to 6.5
- permeability: float32 [2048, 4096], P(('grp', 'sub')), may hold values from 1 to 10
- new_owner: int32 [2048], replicated, may hold values from 0 to 127, as said below
- neighbours: int32 [6, 2048], replicated, may hold values from -1 to 2047, as said below
Outputs:
- new_potential: float32 [3072, 4096], P(('grp', 'sub'))
The draws below stay inside these ranges and needn't reach their ends.
Inputs may be any that keep to these rules, and one draw needn't show every extreme that they name: `new_owner`: owners never fall as the block id rises. Device d's blocks begin at d * 16 + s with s from -4 to 4 (0 for device 0), so each device gets 16 - 2 * 4 to 24 blocks, and some device gets exactly 24. If n = neighbours[f, b] is not -1 then neighbours[f xor 1, n] = b and n lies within 4 of b; the faces 0 and 1 link blocks exactly 4 apart.
All inputs are finite; a program needn't handle non-finite values.
Results may differ from the reference program's by a relative error of at most 0.00024.
Values sent between devices are 32-bit elements; how exact they have to be, the bound alone decides.
A program may use at most 128 MiB of HBM per device.

```python
import math
import jax
import jax.numpy as jnp
from jax import lax

BE = 16
BLK_DEV = 16
CAP = 24
NBLK = 2048
LAYER = 4
NPRE = 2
NPOST = 2
CSWEEP = 4
N_GRP = 8
N_SUB = 16


def draw_new_owner(key, part):
    devices_all = NBLK // BLK_DEV
    shift_len = BLK_DEV // 4
    key_shift, key_place = jax.random.split(jax.random.fold_in(key, 17))
    offsets = jax.random.randint(key_shift, (devices_all + 1,), -shift_len, shift_len + 1)
    widest = jax.random.randint(key_place, (), 1, devices_all - 1)
    index_all = jnp.arange(devices_all + 1, dtype=jnp.int32)
    offsets = jnp.where(index_all == widest, -shift_len, offsets)
    offsets = jnp.where(index_all == widest + 1, shift_len, offsets)
    offsets = jnp.where((index_all == 0) | (index_all == devices_all), 0, offsets)
    bounds = index_all * BLK_DEV + offsets
    blocks = jnp.arange(NBLK, dtype=jnp.int32)
    return jnp.sum((blocks[None, :] >= bounds[1:devices_all, None]).astype(jnp.int32), axis=0).astype(jnp.int32)


def draw_neighbours(key, part):
    cuts = jax.random.randint(jax.random.fold_in(key, 29), (3, NBLK), 0, 4) == 0
    blocks = jnp.arange(NBLK, dtype=jnp.int32)
    inlayer = blocks % 4
    across_x = inlayer % 2
    across_y = inlayer // 2
    layer_index = blocks // 4
    layers_all = NBLK // 4
    upper_z = jnp.where((layer_index < layers_all - 1) & jnp.logical_not(cuts[0]), blocks + 4, -1)
    lower_z = jnp.where((layer_index > 0) & jnp.logical_not(jnp.roll(cuts[0], 4)), blocks - 4, -1)
    upper_y = jnp.where((across_y == 0) & jnp.logical_not(cuts[1]), blocks + 2, -1)
    lower_y = jnp.where((across_y == 1) & jnp.logical_not(jnp.roll(cuts[1], 2)), blocks - 2, -1)
    upper_x = jnp.where((across_x == 0) & jnp.logical_not(cuts[2]), blocks + 1, -1)
    lower_x = jnp.where((across_x == 1) & jnp.logical_not(jnp.roll(cuts[2], 1)), blocks - 1, -1)
    return jnp.stack([lower_z, upper_z, lower_y, upper_y, lower_x, upper_x]).astype(jnp.int32)


def draw_right_side(key, part):
    key_cell, key_block = jax.random.split(jax.random.fold_in(key, 41))
    cells_block = BE * BE * BE
    cells = jnp.clip(jax.random.normal(key_cell, (NBLK, cells_block), jnp.float32), -5.0, 5.0)
    levels = jax.random.uniform(key_block, (NBLK, 1), jnp.float32, -1.5, 1.5)
    return cells + levels


def level_of(own_key, extent, cuts, smallest, top_value):
    factor_of, own = 1.0, jax.random.fold_in(own_key, 6)
    for dim, parts in cuts:
        draws = jnp.exp(jax.random.uniform(jax.random.fold_in(own, dim), (parts,), jnp.float32, smallest / len(cuts), top_value / len(cuts)))
        factor_of = factor_of * jnp.repeat(draws, extent[dim] // parts).reshape([-1 if axis == dim else 1 for axis in range(len(extent))])
    return factor_of


def bell_draw(key, extent, deviation, reach, pieces=(), kind=jnp.bfloat16):
    level = level_of(key, extent, pieces, -0.22, 0.18) if pieces else 1.0
    values = jax.random.normal(key, extent, jnp.float32) * deviation * level
    return jnp.minimum(jnp.maximum(values, -reach), reach).astype(kind)


def setup_inputs(seed: int = 0) -> dict:
    key_of = jax.random.split(jax.random.key(seed), 6)
    potential = bell_draw(key_of[0], (NBLK, BE * BE * BE), 1.0, 6.0, ((0, 128),), jnp.float32)
    right_side = draw_right_side(jax.random.fold_in(key_of[5], 71), 0)
    permeability = jnp.clip(jnp.exp(math.log(10.0) - 2.3025851 * jax.random.uniform(key_of[2], (NBLK, BE * BE * BE), jnp.float32) ** level_of(key_of[2], (NBLK, BE * BE * BE), ((0, 128),), -0.2, 0.2)), 1.0, 10.0)
    new_owner = draw_new_owner(jax.random.fold_in(key_of[5], 71), 0)
    neighbours = draw_neighbours(jax.random.fold_in(key_of[5], 71), 0)
    return dict(potential=potential, right_side=right_side, permeability=permeability, new_owner=new_owner, neighbours=neighbours)


RELAX_FINE = 0.8
RELAX_COARSE = 0.7
OPPOSITE = (1, 0, 3, 2, 5, 4)


def face_one(values, face_index):
    slots_here, block_edge, plane_cells = values.shape
    if face_index == 0:
        return values[:, 0, :]
    if face_index == 1:
        return values[:, block_edge - 1, :]
    if face_index == 2:
        return values[:, :, :block_edge].reshape(slots_here, plane_cells)
    if face_index == 3:
        return values[:, :, plane_cells - block_edge:].reshape(slots_here, plane_cells)
    if face_index == 4:
        return values[:, :, 0::block_edge].reshape(slots_here, plane_cells)
    return values[:, :, block_edge - 1::block_edge].reshape(slots_here, plane_cells)


def face_tiles(values):
    return jnp.stack([face_one(values, face_index) for face_index in range(6)], axis=1)


def beside(values, ghosts):
    slots_here, block_edge, plane_cells = values.shape
    zero_column = jnp.zeros((slots_here, block_edge, 1), values.dtype)
    column_pos = lax.broadcasted_iota(jnp.int32, (1, 1, plane_cells), 2) % block_edge
    lower_z = jnp.concatenate([ghosts[:, 0][:, None, :], values[:, :-1, :]], axis=1)
    upper_z = jnp.concatenate([values[:, 1:, :], ghosts[:, 1][:, None, :]], axis=1)
    lower_y = jnp.concatenate([ghosts[:, 2].reshape(slots_here, block_edge, block_edge), values[:, :, :-block_edge]], axis=2)
    upper_y = jnp.concatenate([values[:, :, block_edge:], ghosts[:, 3].reshape(slots_here, block_edge, block_edge)], axis=2)
    ghost_lower_x = jnp.repeat(ghosts[:, 4].reshape(slots_here, block_edge, block_edge), block_edge, axis=2)
    ghost_upper_x = jnp.repeat(ghosts[:, 5].reshape(slots_here, block_edge, block_edge), block_edge, axis=2)
    lower_x = jnp.where(column_pos == 0, ghost_lower_x, jnp.concatenate([zero_column, values[:, :, :-1]], axis=2))
    upper_x = jnp.where(column_pos == block_edge - 1, ghost_upper_x, jnp.concatenate([values[:, :, 1:], zero_column], axis=2))
    return [lower_z, upper_z, lower_y, upper_y, lower_x, upper_x]


def couplings(perm_field, perm_ghosts):
    return [2.0 * perm_field * nearby / (perm_field + nearby) for nearby in beside(perm_field, perm_ghosts)]


def apply_operator(values, ghosts, coupling, diagonal):
    result = diagonal * values
    for factor, nearby in zip(coupling, beside(values, ghosts)):
        result = result - factor * nearby
    return result


def global_ghosts(face_set, table):
    blocks_total = face_set.shape[0]
    plane_cells = face_set.shape[2]
    flat_tiles = jnp.concatenate([face_set.reshape(blocks_total * 6, plane_cells), jnp.zeros((1, plane_cells), face_set.dtype)], axis=0)
    opposite = jnp.array(OPPOSITE, jnp.int32)[:, None]
    index_rows = jnp.where(table >= 0, table * 6 + opposite, blocks_total * 6)
    return jnp.take(flat_tiles, index_rows.T, axis=0)


def reference(potential, right_side, permeability, new_owner, neighbours):
    plane_cells = BE * BE
    devices_all = N_GRP * N_SUB
    values = potential.reshape(NBLK, BE, plane_cells)
    source = right_side.reshape(NBLK, BE, plane_cells)
    perm_field = permeability.reshape(NBLK, BE, plane_cells)
    boundary = (neighbours < 0).T[:, :, None]
    perm_faces = face_tiles(perm_field)
    perm_ghosts = jnp.where(boundary, perm_faces, global_ghosts(perm_faces, neighbours))
    coupling = couplings(perm_field, perm_ghosts)
    diagonal = coupling[0]
    for factor in coupling[1:]:
        diagonal = diagonal + factor

    def smooth(current):
        ghosts = global_ghosts(face_tiles(current), neighbours)
        return current + RELAX_FINE * (source - apply_operator(current, ghosts, coupling, diagonal)) / diagonal

    for sweep in range(NPRE):
        values = smooth(values)
    residual = source - apply_operator(values, global_ghosts(face_tiles(values), neighbours), coupling, diagonal)
    coarse_rhs = jnp.sum(residual, axis=(1, 2))
    links = jnp.stack([jnp.sum(face_one(coupling[face_index], face_index), axis=1) for face_index in range(6)])
    coarse_diag = jnp.sum(links, axis=0)
    level_shift = jnp.sum(coarse_rhs) / jnp.sum(links)
    padded_len = NBLK + 2 * LAYER + 1
    positions = jnp.where(neighbours >= 0, neighbours + LAYER, padded_len - 1)
    current = jnp.zeros((padded_len,), jnp.float32)
    for sweep in range(CSWEEP):
        inner = current[LAYER:LAYER + NBLK]
        product = coarse_diag * inner - jnp.sum(links * current[positions], axis=0)
        inner = inner + RELAX_COARSE * (coarse_rhs - product) / coarse_diag
        current = jnp.concatenate([jnp.zeros((LAYER,), jnp.float32), inner, jnp.zeros((LAYER + 1,), jnp.float32)])
    correction = current[LAYER:LAYER + NBLK] + level_shift
    values = values + correction[:, None, None]
    for sweep in range(NPOST):
        values = smooth(values)
    bounds = jnp.sum((new_owner[None, :] < jnp.arange(devices_all + 1, dtype=jnp.int32)[:, None]).astype(jnp.int32), axis=1)
    slot_ids = bounds[:devices_all, None] + jnp.arange(CAP, dtype=jnp.int32)[None, :]
    slot_live = slot_ids < bounds[1:, None]
    picked = jnp.take(values.reshape(NBLK, BE * plane_cells), jnp.minimum(slot_ids, NBLK - 1).reshape(-1), axis=0)
    return jnp.where(slot_live.reshape(-1, 1), picked, 0.0)
```

```python
import functools

import jax
import jax.numpy as jnp
from jax import lax
from jax.experimental import pallas as pl
from jax.experimental.pallas import tpu as pltpu
from jax.sharding import PartitionSpec as P

BE = 16
BLK = 16
CAP = 24
LN = 128
RELAX_FINE = 0.8
RELAX_COARSE = 0.7
MESH = pl.DeviceIdType.MESH
F32 = jnp.float32
I32 = jnp.int32
GROUP = (0, 0, 1, 1, 2, 2, 3, 3, 4, 4, 4, 4)
SOURCE = (2, 3, 0, 1, 6, 7, 4, 5)
X_MU, X_U0, X_U1, X_W1, X_U2, X_V1 = range(6)
N_X = 6


def chunk(h):
    return slice(h * LN, (h + 1) * LN)


def steps(n, body, init=None):
    if init is None:
        lax.fori_loop(0, n, lambda i, _: (body(i), 0)[1], 0, unroll=n)
        return None
    return lax.fori_loop(0, n, body, init, unroll=n)


def kernel(
    n_grp, n_sub, nblk,
    pot, rs, mu, owner, neigh, out,
    mu_v, u0_v, rs_v, own_v, nb_v, out_v,
    u, w, cx, cy, cz, dint, t0, inv, coef, rhs, gx, gy, gz, base, base_w,
    own_f, src_f, mu_f, own_mu, ghost, ghost_w, cface, pface, src_w,
    rel, route, bnd, col, qmat, link_w, share_w, corr, rsum,
    send, recv, total, group_total, tail_send, tail_recv, window,
    in_sem, out_sem, x_send, x_recv, l_send, l_recv, s_send, s_recv,
    a_send, a_recv, b_send, b_recv, t_send, t_recv,
):
    grp, sub = lax.axis_index("grp"), lax.axis_index("sub")
    devices = n_grp * n_sub
    me = grp * n_sub + sub

    def dev(by):
        other = lax.rem(me + by + devices, devices)
        return (lax.div(other, n_sub), lax.rem(other, n_sub))

    def in_group(by):
        return (grp, lax.rem(sub + by + n_sub, n_sub))

    def across(by):
        return (lax.rem(grp + by + n_grp, n_grp), sub)

    loads = [
        pltpu.make_async_copy(a, b, in_sem.at[i])
        for i, (a, b) in enumerate(
            ((mu, mu_v), (neigh, nb_v), (pot, u0_v), (rs, rs_v), (owner, own_v))
        )
    ]
    for copy in loads:
        copy.start()

    barrier = pltpu.get_barrier_semaphore()
    for by in (1, -1, 2, -2):
        pl.semaphore_signal(barrier, inc=1, device_id=dev(by), device_id_type=MESH)
    for by in range(1, n_sub):
        pl.semaphore_signal(barrier, inc=1, device_id=in_group(by), device_id_type=MESH)
    for by in range(1, n_grp):
        pl.semaphore_signal(barrier, inc=1, device_id=across(by), device_id_type=MESH)

    lane = lax.broadcasted_iota(I32, (BLK, LN), 1)
    xpos = lane & 15
    yrow = lane >> 4
    row = lax.broadcasted_iota(I32, (BLK, LN), 0)
    lane8 = lax.broadcasted_iota(I32, (8, LN), 1)
    row8 = lax.broadcasted_iota(I32, (8, LN), 0)
    x_first, x_last = xpos == 0, xpos == BE - 1
    x_face = x_first | x_last
    y_first, y_last = lane < BE, lane >= LN - BE
    even = (lane & 1) == 0
    zero = jnp.zeros((BLK, LN), F32)

    def turn(v, by):
        if isinstance(by, int):
            by = by % LN
            return v if by == 0 else pltpu.roll(v, by, 1)
        return pltpu.roll(v, by & (LN - 1), 1)

    def lower_y(v0, v1):
        a, b = turn(v0, BE), turn(v1, BE)
        return a, jnp.where(y_first, a, b)

    def upper_y(v0, v1):
        a, b = turn(v0, -BE), turn(v1, -BE)
        return jnp.where(y_last, b, a), b

    def faces_of(produce, faces_ref, plane):
        for zg in range(2):
            def body(i, carry, zg=zg):
                x0, x1, y2, y3 = carry
                v0, v1 = produce(zg, i)
                here = (xpos == 2 * i) | (xpos == ((2 * i + 15) & 15))
                x0 = jnp.where(here, turn(v0, 2 * i), x0)
                x1 = jnp.where(here, turn(v1, 2 * i), x1)
                line = yrow == i
                y2 = jnp.where(line, turn(v0, BE * i), y2)
                y3 = jnp.where(line, turn(v1, BE * i + BE), y3)
                return x0, x1, y2, y3

            x0, x1, y2, y3 = steps(8, body, (zero, zero, zero, zero))
            faces_ref[8 + 2 * zg] = x0
            faces_ref[9 + 2 * zg] = x1
            faces_ref[4 + zg] = y2
            faces_ref[6 + zg] = y3
        for h in range(2):
            faces_ref[h] = plane(0, h)
            faces_ref[2 + h] = plane(BE - 1, h)

    def sources(faces_ref, src_ref):
        for k in range(12):
            if k < 8:
                v = faces_ref[SOURCE[k]]
            else:
                x = faces_ref[k]
                v = jnp.where(even, turn(x, -15), turn(x, 15))
            src_ref[k, 8:24, :] = v

    def send_faces(src_ref, slot):
        for m in range(6):
            pair = []
            for k in (2 * m, 2 * m + 1):
                edge = jnp.where(row8 < 4, src_ref[k, 8:16, :], src_ref[k, 16:24, :])
                way = route[GROUP[k]]
                d = jnp.zeros((8, LN), F32)
                for r in (4,) if k < 4 else range(1, 8):
                    d = jnp.where(way == r, pltpu.roll(edge, r, 0), d)
                pair.append(d)
            d0, d1 = pair
            send[slot, 0, m] = jnp.where(row8 < 4, d0, pltpu.roll(d1, 4, 0))
            send[slot, 1, m] = jnp.where(row8 < 4, pltpu.roll(d0, 4, 0), d1)
        for copy in face_copies(slot):
            copy.start()

    def face_copies(slot):
        return [
            pltpu.make_async_remote_copy(
                src_ref=send.at[slot, way],
                dst_ref=recv.at[slot, way],
                send_sem=x_send.at[slot, way],
                recv_sem=x_recv.at[slot, way],
                device_id=dev(1 - 2 * way),
                device_id_type=MESH,
            )
            for way in range(2)
        ]

    def local_ghosts(src_ref, ghost_ref):
        for k in range(12):
            r = rel[GROUP[k]]
            g = zero
            for by in (-4, 4) if k < 4 else range(-4, 5):
                g = jnp.where(r == by, src_ref[k, 8 + by : 24 + by, :], g)
            ghost_ref[k] = g

    def add_remote(slot, ghost_ref):
        for copy in face_copies(slot):
            copy.wait_recv()
        for m in range(6):
            lo, hi = recv[slot, 0, m], recv[slot, 1, m]
            lo1, hi0 = pltpu.roll(lo, 4, 0), pltpu.roll(hi, 4, 0)
            ghost_ref[2 * m, 0:8, :] += jnp.where(row8 < 4, lo, 0.0)
            ghost_ref[2 * m + 1, 0:8, :] += jnp.where(row8 < 4, lo1, 0.0)
            ghost_ref[2 * m, 8:16, :] += jnp.where(row8 < 4, 0.0, hi0)
            ghost_ref[2 * m + 1, 8:16, :] += jnp.where(row8 < 4, 0.0, hi)

    def spread_x(faces_ref, zg, i, h):
        return turn(faces_ref[8 + 2 * zg + h], LN - 2 * i)

    def spread_y(faces_ref, zg, i, h):
        return turn(faces_ref[(4, 6)[h] + zg], LN - BE * i - (0, BE)[h])

    first = BLK * me - 24
    loads[1].wait()
    low = lax.div(first + LN, LN) - 1
    shift = first - low * LN
    tiles = nblk // LN

    def table(k):
        at = pl.multiple_of(lax.rem(k + tiles, tiles) * LN, LN)
        rows6 = nb_v[:, pl.ds(at, LN)]
        return jnp.concatenate([rows6, jnp.full((2, LN), -1, I32)], axis=0)

    back = LN - shift
    ta, tb = turn(table(low), back), turn(table(low + 1), back)
    ids = first + lane8
    nb = jnp.where(lane8 < back, ta, tb)
    nb = jnp.where((nb >= 0) & (ids >= 0) & (ids < nblk), nb - first, -1000).astype(F32)
    nbt = nb.T
    col[...] = nbt

    def columns(f, lo, n):
        return jnp.broadcast_to(col[lo : lo + n, f : f + 1], (n, LN))

    rowf = row.astype(F32)
    row8f = row8.astype(F32)
    rels, routes, bnds = [], [], []
    for f in range(6):
        to = columns(f, 24, 16)
        near = (to >= 24.0) & (to < 40.0)
        rels.append(jnp.where(near, to - 24.0 - rowf, 99.0))
        bnds.append(jnp.where(to < 0.0, 1.0, 0.0))
        to8 = jnp.where(row8 < 4, columns(f, 40, 8), columns(f, 16, 8))
        j = jnp.where(row8 < 4, to8 - 32.0, to8 - 24.0)
        ok = jnp.where(row8 < 4, jnp.where(j >= 4.0, 1.0, 0.0), jnp.where(j >= 0.0, 1.0, 0.0))
        ok = ok * jnp.where(row8 < 4, jnp.where(j < 8.0, 1.0, 0.0), jnp.where(j < 4.0, 1.0, 0.0))
        r = row8f - j
        routes.append(jnp.where(ok > 0.5, jnp.where(r < 0.0, r + 8.0, r), 99.0))
    even8 = (lane8 & 1) == 0
    for g in range(4):
        rel[g], route[g], bnd[g] = rels[g], routes[g], bnds[g]
    rel[4] = jnp.where(even, rels[4], rels[5])
    bnd[4] = jnp.where(even, bnds[4], bnds[5])
    route[4] = jnp.where(even8, routes[4], routes[5])

    def plane_of(ref):
        return lambda z, h: ref[:, z * 256 + h * LN : z * 256 + (h + 1) * LN]

    def from_input(ref, store=None):
        def produce(zg, i):
            at = pl.multiple_of((zg * 8 + i) * 256, 256)
            v0, v1 = ref[:, pl.ds(at, LN)], ref[:, pl.ds(at + LN, LN)]
            if store is not None:
                store[zg * 8 + i + 1, :, chunk(0)] = v0
                store[zg * 8 + i + 1, :, chunk(1)] = v1
            return v0, v1

        return produce

    loads[0].wait()
    faces_of(from_input(mu_v), own_mu, plane_of(mu_v))
    sources(own_mu, src_w)
    pl.semaphore_wait(barrier, 4 + n_sub - 1 + n_grp - 1)
    send_faces(src_w, X_MU)
    loads[2].wait()
    faces_of(from_input(u0_v, u), own_f, plane_of(u0_v))
    sources(own_f, src_f)
    send_faces(src_f, X_U0)

    local_ghosts(src_w, mu_f)
    local_ghosts(src_f, ghost)
    for ref in (u, w):
        ref[0] = jnp.zeros((BLK, 256), F32)
        ref[BE + 1] = jnp.zeros((BLK, 256), F32)
    cz[0] = jnp.zeros((BLK, 256), F32)
    cz[BE] = jnp.zeros((BLK, 256), F32)

    def mean(a, b):
        return 2.0 * a * b / (a + b)

    def inner_couplings(z):
        at = pl.multiple_of(z * 256, 256)
        m0, m1 = mu_v[:, pl.ds(at, LN)], mu_v[:, pl.ds(at + LN, LN)]
        y0, y1 = lower_y(m0, m1)
        cx[z, :, chunk(0)] = jnp.where(x_first, 0.0, mean(m0, turn(m0, 1)))
        cx[z, :, chunk(1)] = jnp.where(x_first, 0.0, mean(m1, turn(m1, 1)))
        cy[z, :, chunk(0)] = jnp.where(y_first, 0.0, mean(m0, y0))
        cy[z, :, chunk(1)] = mean(m1, y1)

    def z_couplings(z):
        at = pl.multiple_of(z * 256, 256)
        a = mu_v[:, pl.ds(at, 256)]
        b = mu_v[:, pl.ds(at + 256, 256)]
        cz[z + 1] = mean(a, b)

    steps(BE, inner_couplings)
    steps(BE - 1, z_couplings)
    loads[3].wait()

    def around(z):
        cx0, cx1 = cx[z, :, chunk(0)], cx[z, :, chunk(1)]
        cy0, cy1 = cy[z, :, chunk(0)], cy[z, :, chunk(1)]
        uy0, uy1 = upper_y(cy0, cy1)
        uy1 = jnp.where(y_last, 0.0, uy1)
        lo = (cz[z, :, chunk(0)], cz[z, :, chunk(1)])
        up = (cz[z + 1, :, chunk(0)], cz[z + 1, :, chunk(1)])
        return (
            (lo[0], up[0], cy0, uy0, cx0, turn(cx0, -1)),
            (lo[1], up[1], cy1, uy1, cx1, turn(cx1, -1)),
        )

    def beside(ref, z):
        v0, v1 = ref[z + 1, :, chunk(0)], ref[z + 1, :, chunk(1)]
        l0, l1 = lower_y(v0, v1)
        p0, p1 = upper_y(v0, v1)
        return (v0, v1), (
            (ref[z, :, chunk(0)], ref[z + 2, :, chunk(0)], l0, p0, turn(v0, 1), turn(v0, -1)),
            (ref[z, :, chunk(1)], ref[z + 2, :, chunk(1)], l1, p1, turn(v1, 1), turn(v1, -1)),
        )

    def first_terms(z, acc):
        c = around(z)
        _, n = beside(u, z)
        for h in range(2):
            at = pl.multiple_of(z * 256 + h * LN, LN)
            r = rs_v[:, pl.ds(at, LN)]
            d = c[h][0]
            t = r + c[h][0] * n[h][0]
            for f in range(1, 6):
                d = d + c[h][f]
                t = t + c[h][f] * n[h][f]
            dint[z, :, chunk(h)] = d
            t0[z, :, chunk(h)] = t
            acc = acc + r
        return acc

    acc = steps(BE, first_terms, zero)
    rsum[...] = jnp.broadcast_to(jnp.sum(acc, axis=1, keepdims=True), (BLK, LN))

    add_remote(X_MU, mu_f)
    for k in range(12):
        m = own_mu[k]
        g = jnp.where(bnd[GROUP[k]] > 0.5, m, mu_f[k])
        cface[k] = mean(m, g)
    for h in range(2):
        dint[0, :, chunk(h)] += cface[h]
        dint[BE - 1, :, chunk(h)] += cface[2 + h]
    add_remote(X_U0, ghost)
    for k in range(12):
        pface[k] = cface[k] * ghost[k]
    for h in range(2):
        t0[0, :, chunk(h)] += pface[h]
        t0[BE - 1, :, chunk(h)] += pface[2 + h]

    y_face = (y_first, y_last)

    def sweep_first(zg, i):
        z = zg * 8 + i
        vs = []
        for h in range(2):
            d = dint[z, :, chunk(h)]
            t = t0[z, :, chunk(h)]
            d = d + jnp.where(x_face, spread_x(cface, zg, i, h), 0.0)
            d = d + jnp.where(y_face[h], spread_y(cface, zg, i, h), 0.0)
            t = t + jnp.where(x_face, spread_x(pface, zg, i, h), 0.0)
            t = t + jnp.where(y_face[h], spread_y(pface, zg, i, h), 0.0)
            q = RELAX_FINE / d
            inv[z, :, chunk(h)] = q
            v = (1.0 - RELAX_FINE) * u[z + 1, :, chunk(h)] + q * t
            u[z + 1, :, chunk(h)] = v
            vs.append(v)
        return vs

    def plane_u(ref):
        return lambda z, h: ref[z + 1, :, chunk(h)]

    faces_of(sweep_first, own_f, plane_u(u))
    sources(own_f, src_f)
    send_faces(src_f, X_U1)

    bx = jnp.where(x_first, bnds[4], jnp.where(x_last, bnds[5], 0.0))
    by_ = (jnp.where(y_first, bnd[2], 0.0), jnp.where(y_last, bnd[3], 0.0))

    for h in range(2):
        gz[0, :, chunk(h)] = cface[h] * inv[0, :, chunk(h)]
        gz[1, :, chunk(h)] = cface[2 + h] * inv[BE - 1, :, chunk(h)]

    def coefficients(zg, i):
        z = zg * 8 + i
        c = around(z)
        vs = []
        for h in range(2):
            q = inv[z, :, chunk(h)]
            for f in range(6):
                coef[f, z, :, chunk(h)] = c[h][f] * q
            at = pl.multiple_of(z * 256 + h * LN, LN)
            rhs[z, :, chunk(h)] = rs_v[:, pl.ds(at, LN)] * q
            fx = jnp.where(x_face, spread_x(cface, zg, i, h), 0.0) * q
            fy = jnp.where(y_face[h], spread_y(cface, zg, i, h), 0.0) * q
            gx[z, :, chunk(h)] = fx
            gy[z, :, chunk(h)] = fy
            v = 1.0 - fx * bx - fy * by_[h]
            w[z + 1, :, chunk(h)] = v
            vs.append(v)
        return vs

    for zg in range(2):
        steps(8, lambda i, zg=zg: (coefficients(zg, i), None)[1])

    def inner_sweep(ref, base_ref, with_rhs):
        def body(z):
            v, n = beside(ref, z)
            for h in range(2):
                b = (1.0 - RELAX_FINE) * v[h]
                if with_rhs:
                    b = b + rhs[z, :, chunk(h)]
                for f in range(6):
                    b = b + coef[f, z, :, chunk(h)] * n[h][f]
                base_ref[z, :, chunk(h)] = b

        steps(BE, body)

    def add_z(ghost_ref, base_ref):
        for h in range(2):
            base_ref[0, :, chunk(h)] += gz[0, :, chunk(h)] * ghost_ref[h]
            base_ref[BE - 1, :, chunk(h)] += gz[1, :, chunk(h)] * ghost_ref[2 + h]

    def outer_sweep(ghost_ref, base_ref, ref):
        def produce(zg, i):
            z = zg * 8 + i
            vs = []
            for h in range(2):
                v = base_ref[z, :, chunk(h)]
                v = v + gx[z, :, chunk(h)] * spread_x(ghost_ref, zg, i, h)
                v = v + gy[z, :, chunk(h)] * spread_y(ghost_ref, zg, i, h)
                ref[z + 1, :, chunk(h)] = v
                vs.append(v)
            return vs

        return produce

    inner_sweep(u, base, True)
    local_ghosts(src_f, ghost)

    def face_sums(value):
        sums = []
        for f in range(4):
            s = value(2 * f) + value(2 * f + 1)
            sums.append(jnp.sum(s, axis=1, keepdims=True))
        s = value(8) + value(9) + value(10) + value(11)
        sums.append(jnp.sum(jnp.where(even, s, 0.0), axis=1, keepdims=True))
        sums.append(jnp.sum(jnp.where(even, 0.0, s), axis=1, keepdims=True))
        return sums

    links = face_sums(lambda k: cface[k])
    tile = zero
    link_total = links[0]
    for f in range(6):
        tile = jnp.where(lane == f, links[f], tile)
        if f:
            link_total = link_total + links[f]
    link_w[24:40] = tile
    link_w[0:8] = jnp.ones((8, LN), F32)
    link_w[56:64] = jnp.ones((8, LN), F32)

    def remote(src, dst, a, b, to):
        return pltpu.make_async_remote_copy(
            src_ref=src, dst_ref=dst, send_sem=a, recv_sem=b, device_id=to, device_id_type=MESH
        )

    def two_way(ref, a, b):
        return [
            remote(ref.at[pl.ds(24, 16)], ref.at[pl.ds(8, 16)], a.at[0], b.at[0], dev(1)),
            remote(ref.at[pl.ds(24, 16)], ref.at[pl.ds(40, 16)], a.at[1], b.at[1], dev(-1)),
        ]

    link_copies = two_way(link_w, l_send, l_recv)
    for copy in link_copies:
        copy.start()

    for h in range(2):
        w[1, :, chunk(h)] -= gz[0, :, chunk(h)] * bnd[0]
        w[BE, :, chunk(h)] -= gz[1, :, chunk(h)] * bnd[1]

    def from_w(zg, i):
        z = zg * 8 + i
        return w[z + 1, :, chunk(0)], w[z + 1, :, chunk(1)]

    faces_of(from_w, own_mu, plane_u(w))
    sources(own_mu, src_w)
    send_faces(src_w, X_W1)

    add_remote(X_U1, ghost)
    add_z(ghost, base)
    faces_of(outer_sweep(ghost, base, u), own_f, plane_u(u))
    sources(own_f, src_f)
    send_faces(src_f, X_U2)

    sums = face_sums(lambda k: cface[k] * own_f[k])
    left = rsum[:, 0:1]
    group_left = left
    tile = zero
    for f in range(6):
        tile = jnp.where(lane == f, sums[f], tile)
        left = left - sums[f]
        group_left = group_left - sums[f] * bnds[f][:, 0:1]
    share_w[24:40] = jnp.where(lane == 6, left, tile)
    share_copies = two_way(share_w, s_send, s_recv) + [
        remote(
            share_w.at[pl.ds(32, 8)], share_w.at[pl.ds(0, 8)], s_send.at[2], s_recv.at[2], dev(2)
        ),
        remote(
            share_w.at[pl.ds(24, 8)], share_w.at[pl.ds(56, 8)], s_send.at[3], s_recv.at[3], dev(-2)
        ),
    ]
    for copy in share_copies:
        copy.start()
    total[0] = jnp.where(
        lane8 < 64,
        jnp.sum(group_left, axis=0, keepdims=True),
        jnp.sum(link_total, axis=0, keepdims=True),
    )
    total_copies = [
        remote(total.at[0], total.at[i], a_send.at[i], a_recv.at[i], in_group(i))
        for i in range(1, n_sub)
    ]
    for copy in total_copies:
        copy.start()

    inner_sweep(u, base, True)
    local_ghosts(src_f, ghost)
    for copy in link_copies:
        copy.wait_recv()
    i64 = lax.broadcasted_iota(I32, (64, 64), 0)
    l64 = lax.broadcasted_iota(I32, (64, 64), 1)
    l64f = l64.astype(F32)
    diagonal = link_w[:, 0:1]
    for f in range(1, 6):
        diagonal = diagonal + link_w[:, f : f + 1]
    gain = RELAX_COARSE / diagonal
    ident = jnp.where(i64 == l64, 1.0, 0.0)
    hot = [jnp.where(col[0:64, f : f + 1] == l64f, 1.0, 0.0) for f in range(6)]
    gmat = link_w[:, 0:1] * hot[0]
    for f in range(1, 6):
        gmat = gmat + link_w[:, f : f + 1] * hot[f]
    gmat = gmat * gain + (1.0 - RELAX_COARSE) * ident

    def product(a, b):
        return lax.dot_general(
            a,
            b,
            (((1,), (0,)), ((), ())),
            precision=lax.Precision.HIGHEST,
            preferred_element_type=F32,
        )

    ymat = ident + gmat
    ymat = ident + product(ymat, gmat)
    ymat = ident + product(ymat, gmat)
    scale = jnp.sum(ident * gain, axis=0, keepdims=True)
    picks = jnp.concatenate([ident[24:40]] + [hot[f][24:40] for f in range(6)], axis=0)
    qmat[...] = product(picks, ymat) * scale

    inner_sweep(w, base_w, False)
    local_ghosts(src_w, ghost_w)
    add_remote(X_W1, ghost_w)
    add_z(ghost_w, base_w)
    finish_w = outer_sweep(ghost_w, base_w, w)
    for zg in range(2):
        steps(8, lambda i, zg=zg: (finish_w(zg, i), None)[1])

    for copy in share_copies:
        copy.wait_recv()
    acc = ident * share_w[:, 6:7]
    i64f = i64.astype(F32)
    for f in range(6):
        acc = acc + jnp.where(nb[f : f + 1, 0:64] == i64f, share_w[:, (f ^ 1) : (f ^ 1) + 1], 0.0)
    source_row = jnp.sum(acc, axis=0, keepdims=True)
    fixed = jnp.sum(qmat[...] * source_row, axis=1, keepdims=True)
    own_fix = fixed[0:16]
    corr[0] = jnp.broadcast_to(own_fix, (BLK, LN))
    for f in range(6):
        corr[1 + f] = jnp.broadcast_to(fixed[16 + 16 * f : 32 + 16 * f] - own_fix, (BLK, LN))
    fix_x = jnp.where(even, corr[5], corr[6])

    add_remote(X_U2, ghost)
    for k in range(12):
        ghost[k] += corr[1 + GROUP[k]] if k < 8 else fix_x
    add_z(ghost, base)
    third = outer_sweep(ghost, base, u)

    def third_sweep(zg, i):
        z = zg * 8 + i
        vs = third(zg, i)
        vs = [vs[h] + corr[0] for h in range(2)]
        for h in range(2):
            u[z + 1, :, chunk(h)] = vs[h]
        return vs

    faces_of(third_sweep, own_f, plane_u(u))
    sources(own_f, src_f)
    send_faces(src_f, X_V1)

    for copy in total_copies:
        copy.wait_recv()
    part = total[0]
    for i in range(1, n_sub):
        part = part + total[i]
    group_total[0] = part
    group_copies = [
        remote(group_total.at[0], group_total.at[i], b_send.at[i], b_recv.at[i], across(i))
        for i in range(1, n_grp)
    ]
    for copy in group_copies:
        copy.start()

    inner_sweep(u, base, True)
    local_ghosts(src_f, ghost)
    for copy in group_copies:
        copy.wait_recv()
    part = group_total[0]
    for i in range(1, n_grp):
        part = part + group_total[i]
    level = part[0:1, 0:1] / part[0:1, 64:65]
    level = jnp.broadcast_to(level, (BLK, LN))

    add_remote(X_V1, ghost)
    add_z(ghost, base)
    tail_copies = []
    for zg in range(2):
        def last_sweep(i, zg=zg):
            z = zg * 8 + i
            vs = []
            for h in range(2):
                v = base[z, :, chunk(h)] + level * w[z + 1, :, chunk(h)]
                v = v + gx[z, :, chunk(h)] * spread_x(ghost, zg, i, h)
                v = v + gy[z, :, chunk(h)] * spread_y(ghost, zg, i, h)
                window[2 * z + h, 8:24, :] = v
                vs.append(v)
            v0, v1 = vs
            tail_send[0, z] = jnp.where(row8 < 4, pltpu.roll(v0[8:16], 4, 0), v1[8:16])
            tail_send[1, z] = jnp.where(row8 < 4, v0[0:8], pltpu.roll(v1[0:8], 4, 0))

        steps(8, last_sweep)
        for way in range(2):
            copy = remote(
                tail_send.at[way, pl.ds(8 * zg, 8)],
                tail_recv.at[way, pl.ds(8 * zg, 8)],
                t_send.at[way, zg],
                t_recv.at[way, zg],
                dev(1 - 2 * way),
            )
            copy.start()
            tail_copies.append(copy)

    loads[4].wait()
    owners = own_v[...]
    starts = jnp.sum(jnp.where(owners < me, 1.0, 0.0)).astype(I32)
    count = jnp.sum(jnp.where(owners == me, 1.0, 0.0)).astype(I32)
    at = jnp.clip(starts - BLK * me + 8, 4, 12)
    row24 = lax.broadcasted_iota(I32, (CAP, LN), 0)
    live = row24 < count
    out_copies = []
    for zg in range(2):
        for copy in tail_copies[2 * zg : 2 * zg + 2]:
            copy.wait_recv()

        def place(i, zg=zg):
            z = zg * 8 + i
            lo, hi = tail_recv[0, z], tail_recv[1, z]
            window[2 * z, 0:8, :] = pltpu.roll(lo, 4, 0)
            window[2 * z + 1, 0:8, :] = lo
            window[2 * z, 24:32, :] = hi
            window[2 * z + 1, 24:32, :] = pltpu.roll(hi, 4, 0)

        steps(8, place)

        def emit(i, zg=zg):
            z = zg * 8 + i
            for h in range(2):
                lanes = pl.ds(pl.multiple_of(z * 256 + h * LN, LN), LN)
                out_v[:, lanes] = jnp.where(live, window[2 * z + h, pl.ds(at, CAP), :], 0.0)

        steps(8, emit)
        half = pl.ds(zg * 2048, 2048)
        copy = pltpu.make_async_copy(out_v.at[:, half], out.at[:, half], out_sem.at[zg])
        copy.start()
        out_copies.append(copy)

    for slot in range(N_X):
        for copy in face_copies(slot):
            copy.wait_send()
    for copy in link_copies + share_copies + total_copies + group_copies + tail_copies:
        copy.wait_send()
    for copy in out_copies:
        copy.wait()


def local(potential, right_side, permeability, new_owner, neighbours):
    n_grp, n_sub = lax.axis_size("grp"), lax.axis_size("sub")
    nblk = new_owner.shape[0]
    vmem = pltpu.VMEM
    plane = (BLK, 256)
    dma = pltpu.SemaphoreType.DMA
    scratch = [
        vmem((BLK, 4096), F32),
        vmem((BLK, 4096), F32),
        vmem((BLK, 4096), F32),
        vmem((nblk // LN, LN), I32),
        vmem((6, nblk), I32),
        vmem((CAP, 4096), F32),
        vmem((BE + 2, *plane), F32),
        vmem((BE + 2, *plane), F32),
        vmem((BE, *plane), F32),
        vmem((BE, *plane), F32),
        vmem((BE + 1, *plane), F32),
        vmem((BE, *plane), F32),
        vmem((BE, *plane), F32),
        vmem((BE, *plane), F32),
        vmem((6, BE, *plane), F32),
        vmem((BE, *plane), F32),
        vmem((BE, *plane), F32),
        vmem((BE, *plane), F32),
        vmem((2, *plane), F32),
        vmem((BE, *plane), F32),
        vmem((BE, *plane), F32),
        vmem((12, BLK, LN), F32),
        vmem((12, 32, LN), F32),
        vmem((12, BLK, LN), F32),
        vmem((12, BLK, LN), F32),
        vmem((12, BLK, LN), F32),
        vmem((12, BLK, LN), F32),
        vmem((12, BLK, LN), F32),
        vmem((12, BLK, LN), F32),
        vmem((12, 32, LN), F32),
        vmem((5, BLK, LN), F32),
        vmem((5, 8, LN), F32),
        vmem((5, BLK, LN), F32),
        vmem((LN, 8), F32),
        vmem((112, 64), F32),
        vmem((64, LN), F32),
        vmem((64, LN), F32),
        vmem((7, BLK, LN), F32),
        vmem((BLK, LN), F32),
        vmem((N_X, 2, 6, 8, LN), F32),
        vmem((N_X, 2, 6, 8, LN), F32),
        vmem((n_sub, 8, LN), F32),
        vmem((n_grp, 8, LN), F32),
        vmem((2, BE, 8, LN), F32),
        vmem((2, BE, 8, LN), F32),
        vmem((32, 40, LN), F32),
        dma((5,)),
        dma((2,)),
        dma((N_X, 2)),
        dma((N_X, 2)),
        dma((2,)),
        dma((2,)),
        dma((4,)),
        dma((4,)),
        dma((n_sub,)),
        dma((n_sub,)),
        dma((n_grp,)),
        dma((n_grp,)),
        dma((2, 2)),
        dma((2, 2)),
    ]
    return pl.pallas_call(
        functools.partial(kernel, n_grp, n_sub, nblk),
        out_shape=jax.ShapeDtypeStruct((CAP, 4096), F32),
        in_specs=[pl.BlockSpec(memory_space=pl.ANY)] * 5,
        out_specs=pl.BlockSpec(memory_space=pl.ANY),
        scratch_shapes=scratch,
        compiler_params=pltpu.CompilerParams(
            collective_id=0, has_side_effects=True, vmem_limit_bytes=32 * 1024 * 1024
        ),
        cost_estimate=pl.CostEstimate(
            flops=8_000_000, bytes_accessed=1_200_000, transcendentals=0
        ),
        name="cycle",
    )(potential, right_side, permeability, new_owner.reshape(nblk // LN, LN), neighbours)


def solution(mesh):
    in_specs = (P(("grp", "sub"), None), P(("grp", "sub"), None), P(("grp", "sub"), None), P(), P())
    out_specs = P(("grp", "sub"), None)
    return jax.shard_map(local, mesh=mesh, in_specs=in_specs, out_specs=out_specs, check_vma=False)
```

```python
import functools
import types

import jax
import jax.numpy as jnp
from jax import lax
from jax.experimental import pallas as pl
from jax.experimental.pallas import tpu as pltpu
from jax.sharding import PartitionSpec as P

BE = 16
BLK = 16
CAP = 24
LN = 128
RELAX_FINE = 0.8
RELAX_COARSE = 0.7
MESH = pl.DeviceIdType.MESH
F32 = jnp.float32
I32 = jnp.int32
GROUP = (0, 0, 1, 1, 2, 2, 3, 3, 4, 4, 4, 4)
SOURCE = (2, 3, 0, 1, 6, 7, 4, 5)
X_MU, X_U0, X_U1, X_U2 = range(4)
N_X = 4
WIN = 80
MINE = 32


def chunk(h):
    return slice(h * LN, (h + 1) * LN)


def steps(n, body, init=None):
    if init is None:
        lax.fori_loop(0, n, lambda i, _: (body(i), 0)[1], 0, unroll=n)
        return None
    return lax.fori_loop(0, n, body, init, unroll=n)


def kernel(
    n_grp, n_sub, nblk,
    pot, rs, mu, owner, neigh, out,
    mu_s, u0_s, rs_s, own_v, nb_v,
    u_s, w_s, cx_s, cy_s, cz_s, dint_s, t0_s, inv_s, coef_s, rhs_s, gx_s, gy_s, gz_s, base_s, base_w_s,
    faces_s, wfaces_s, ghost_s, cface_s, rel_s, bnd_s, corr_s,
    pface, mu_f, own_mu, src_f, src_w, near_local, near_far, keep,
    rel_local, route, col, qmat, link_w, share_w, rsum,
    send, recv, total, group_total, window,
    in_sem, x_send, x_recv, l_send, l_recv, s_send, s_recv,
    a_send, a_recv, b_send, b_recv, k_send, k_recv, g_send, g_recv, c_send, c_recv,
):
    def state(k):
        return types.SimpleNamespace(
            mu_v=mu_s.at[k], u0_v=u0_s.at[k], rs_v=rs_s.at[k], u=u_s.at[k], w=w_s.at[k],
            cx=cx_s.at[k], cy=cy_s.at[k], cz=cz_s.at[k], dint=dint_s.at[k], t0=t0_s.at[k],
            inv=inv_s.at[k], coef=coef_s.at[k], rhs=rhs_s.at[k], gx=gx_s.at[k], gy=gy_s.at[k],
            gz=gz_s.at[k], base=base_s.at[k], base_w=base_w_s.at[k], faces=faces_s.at[k],
            wfaces=wfaces_s.at[k], ghost=ghost_s.at[k], cface=cface_s.at[k], rel=rel_s.at[k],
            bnd=bnd_s.at[k], corr=corr_s.at[k],
        )

    own, rim = state(0), state(1)
    both = (own, rim)
    grp, sub = lax.axis_index("grp"), lax.axis_index("sub")
    devices = n_grp * n_sub
    me = grp * n_sub + sub

    def dev(by):
        other = lax.rem(me + by + devices, devices)
        return (lax.div(other, n_sub), lax.rem(other, n_sub))

    def in_group(by):
        return (grp, lax.rem(sub + by + n_sub, n_sub))

    def across(by):
        return (lax.rem(grp + by + n_grp, n_grp), sub)

    def has(by):
        return (me + by >= 0) & (me + by < devices)

    barrier = pltpu.get_barrier_semaphore()

    def greet(to):
        pl.semaphore_signal(barrier, inc=1, device_id=to, device_id_type=MESH)

    greeted = n_sub - 1 + n_grp - 1
    for by in (1, -1, 2, -2):
        pl.when(has(by))(functools.partial(greet, dev(by)))
        greeted = greeted + has(by).astype(I32)
    for by in range(1, n_sub):
        greet(in_group(by))
    for by in range(1, n_grp):
        greet(across(by))

    loads = [
        pltpu.make_async_copy(a, b, in_sem.at[i])
        for i, (a, b) in enumerate(
            ((mu, own.mu_v), (neigh, nb_v), (pot, own.u0_v), (rs, own.rs_v), (owner, own_v))
        )
    ]
    for copy in loads:
        copy.start()

    lane = lax.broadcasted_iota(I32, (BLK, LN), 1)
    xpos = lane & 15
    yrow = lane >> 4
    row = lax.broadcasted_iota(I32, (BLK, LN), 0)
    lane8 = lax.broadcasted_iota(I32, (8, LN), 1)
    row8 = lax.broadcasted_iota(I32, (8, LN), 0)
    x_first, x_last = xpos == 0, xpos == BE - 1
    x_face = x_first | x_last
    y_first, y_last = lane < BE, lane >= LN - BE
    even = (lane & 1) == 0
    zero = jnp.zeros((BLK, LN), F32)

    def turn(v, by):
        if isinstance(by, int):
            by = by % LN
            return v if by == 0 else pltpu.roll(v, by, 1)
        return pltpu.roll(v, by & (LN - 1), 1)

    def lower_y(v0, v1):
        a, b = turn(v0, BE), turn(v1, BE)
        return a, jnp.where(y_first, a, b)

    def upper_y(v0, v1):
        a, b = turn(v0, -BE), turn(v1, -BE)
        return jnp.where(y_last, b, a), b

    def remote(src, dst, a, b, to):
        return pltpu.make_async_remote_copy(
            src_ref=src, dst_ref=dst, send_sem=a, recv_sem=b, device_id=to, device_id_type=MESH
        )

    def faces_of(produce, faces_ref, plane):
        for zg in range(2):
            def body(i, carry, zg=zg):
                x0, x1, y2, y3 = carry
                v0, v1 = produce(zg, i)
                here = (xpos == 2 * i) | (xpos == ((2 * i + 15) & 15))
                x0 = jnp.where(here, turn(v0, 2 * i), x0)
                x1 = jnp.where(here, turn(v1, 2 * i), x1)
                line = yrow == i
                y2 = jnp.where(line, turn(v0, BE * i), y2)
                y3 = jnp.where(line, turn(v1, BE * i + BE), y3)
                return x0, x1, y2, y3

            x0, x1, y2, y3 = steps(8, body, (zero, zero, zero, zero))
            faces_ref[8 + 2 * zg] = x0
            faces_ref[9 + 2 * zg] = x1
            faces_ref[4 + zg] = y2
            faces_ref[6 + zg] = y3
        for h in range(2):
            faces_ref[h] = plane(0, h)
            faces_ref[2 + h] = plane(BE - 1, h)

    def sources(faces_ref, src_ref, is_rim=False):
        for k in range(12):
            if k < 8:
                v = faces_ref[SOURCE[k]]
            else:
                x = faces_ref[k]
                v = jnp.where(even, turn(x, -15), turn(x, 15))
            if is_rim:
                src_ref[k, 8:16, :] = v[0:8]
                src_ref[k, 32:40, :] = v[8:16]
            else:
                src_ref[k, 16:32, :] = v

    def send_faces(src_ref, slot):
        for m in range(6):
            pair = []
            for k in (2 * m, 2 * m + 1):
                edge = jnp.where(row8 < 4, src_ref[k, 16:24, :], src_ref[k, 24:32, :])
                way = route[GROUP[k]]
                d = jnp.zeros((8, LN), F32)
                for r in (4,) if k < 4 else range(1, 8):
                    d = jnp.where(way == r, pltpu.roll(edge, r, 0), d)
                pair.append(d)
                if slot:
                    keep[slot - 1, k] = d
            d0, d1 = pair
            send[slot, 0, m] = jnp.where(row8 < 4, d0, pltpu.roll(d1, 4, 0))
            send[slot, 1, m] = jnp.where(row8 < 4, pltpu.roll(d0, 4, 0), d1)
        start(face_copies(slot))

    def face_copies(slot):
        return [
            (
                remote(
                    send.at[slot, way],
                    recv.at[slot, way],
                    x_send.at[slot, way],
                    x_recv.at[slot, way],
                    dev(1 - 2 * way),
                ),
                1 - 2 * way,
            )
            for way in range(2)
        ]

    def local_ghosts(src_ref, ghost_ref):
        for k in range(12):
            r = rel_local[GROUP[k]]
            g = zero
            for by in (-4, 4) if k < 4 else range(-4, 5):
                g = jnp.where(r == by, src_ref[k, 16 + by : 32 + by, :], g)
            ghost_ref[k] = g

    def all_ghosts(src_ref, st):
        for k in range(12):
            r = st.rel[GROUP[k]]
            tops = (8, 32) if st is rim else (16, 24)
            for t in range(2):
                g = jnp.zeros((8, LN), F32)
                rt = r[8 * t : 8 * t + 8]
                for by in (-4, 4) if k < 4 else range(-4, 5):
                    g = jnp.where(rt == by, src_ref[k, tops[t] + by : tops[t] + by + 8, :], g)
                st.ghost[k, 8 * t : 8 * t + 8, :] = g

    def add_remote(slot, near_ref, ghost_ref):
        arrive(face_copies(slot))
        for m in range(6):
            lo, hi = recv[slot, 0, m], recv[slot, 1, m]
            lo1, hi0 = pltpu.roll(lo, 4, 0), pltpu.roll(hi, 4, 0)
            a, b = 2 * m, 2 * m + 1
            ghost_ref[a, 0:8, :] = near_ref[a, 0:8, :] + jnp.where(row8 < 4, lo, 0.0)
            ghost_ref[b, 0:8, :] = near_ref[b, 0:8, :] + jnp.where(row8 < 4, lo1, 0.0)
            ghost_ref[a, 8:16, :] = near_ref[a, 8:16, :] + jnp.where(row8 < 4, 0.0, hi0)
            ghost_ref[b, 8:16, :] = near_ref[b, 8:16, :] + jnp.where(row8 < 4, 0.0, hi)

    def rows_both_ways(src, dst, a, b):
        return [
            (remote(src(8), dst(0), a.at[0], b.at[0], dev(1)), 1),
            (remote(src(0), dst(8), a.at[1], b.at[1], dev(-1)), -1),
        ]

    def field_copies(k):
        ref = (mu_s, u0_s, rs_s)[k]
        return rows_both_ways(
            lambda r: ref.at[0, pl.ds(r, 8)],
            lambda r: ref.at[1, pl.ds(r, 8)],
            k_send.at[k],
            k_recv.at[k],
        )

    def ghost_copies(slot):
        return rows_both_ways(
            lambda r: near_local.at[slot, :, pl.ds(r, 8)],
            lambda r: near_far.at[slot, :, pl.ds(r, 8)],
            g_send.at[slot],
            g_recv.at[slot],
        )

    def coupling_copies():
        return rows_both_ways(
            lambda r: cface_s.at[0, :, pl.ds(r, 8)],
            lambda r: cface_s.at[1, :, pl.ds(r, 8)],
            c_send,
            c_recv,
        )

    def start(copies):
        for copy, by in copies:
            if by is None:
                copy.start()
            else:
                pl.when(has(by))(copy.start)

    def arrive(copies):
        for copy, by in copies:
            if by is None:
                copy.wait_recv()
            else:
                pl.when(has(-by))(copy.wait_recv)

    def finish(copies):
        for copy, by in copies:
            if by is None:
                copy.wait_send()
            else:
                pl.when(has(by))(copy.wait_send)

    def rim_ghosts(slot):
        arrive(ghost_copies(slot))
        for k in range(12):
            d = keep[slot, k]
            rim.ghost[k, 0:8, :] = near_far[slot, k, 0:8, :] + jnp.where(row8 < 4, 0.0, d)
            rim.ghost[k, 8:16, :] = near_far[slot, k, 8:16, :] + jnp.where(row8 < 4, d, 0.0)

    def spread_x(faces_ref, zg, i, h):
        return turn(faces_ref[8 + 2 * zg + h], LN - 2 * i)

    def spread_y(faces_ref, zg, i, h):
        return turn(faces_ref[(4, 6)[h] + zg], LN - BE * i - (0, BE)[h])

    first = BLK * me - MINE
    loads[1].wait()
    low = lax.div(first + LN, LN) - 1
    shift = first - low * LN
    tiles = nblk // LN

    def table(k):
        at = pl.multiple_of(lax.rem(k + tiles, tiles) * LN, LN)
        rows6 = nb_v[:, pl.ds(at, LN)]
        return jnp.concatenate([rows6, jnp.full((2, LN), -1, I32)], axis=0)

    back = LN - shift
    ta, tb = turn(table(low), back), turn(table(low + 1), back)
    ids = first + lane8
    nb = jnp.where(lane8 < back, ta, tb)
    nb = jnp.where((nb >= 0) & (ids >= 0) & (ids < nblk), nb - first, -1000).astype(F32)
    nbt = nb.T
    col[...] = nbt

    def columns(f, lo, n):
        return jnp.broadcast_to(col[lo : lo + n, f : f + 1], (n, LN))

    rowf = row.astype(F32)
    row8f = row8.astype(F32)
    rim_row = jnp.where(row < 8, rowf + (MINE - 8.0), rowf + (MINE + 8.0))
    far = jnp.zeros((BLK, LN), F32) + 99.0
    rels, routes, edges, full, rim_full, rim_edges = [], [], [], [], [], []
    for f in range(6):
        to = columns(f, MINE, 16)
        step = to - float(MINE) - rowf
        near = (to >= float(MINE)) & (to < MINE + 16.0)
        rels.append(jnp.where(near, step, far))
        full.append(step)
        edges.append(jnp.where(to < 0.0, 1.0, 0.0))
        before, after = columns(f, MINE - 8, 8), columns(f, MINE + 16, 8)
        to = jnp.concatenate([before, after], axis=0)
        rim_full.append(to - rim_row)
        rim_edges.append(jnp.where(to < 0.0, 1.0, 0.0))
        to8 = jnp.where(row8 < 4, after, before)
        j = jnp.where(row8 < 4, to8 - (MINE + 8.0), to8 - float(MINE))
        ok = jnp.where(row8 < 4, jnp.where(j >= 4.0, 1.0, 0.0), jnp.where(j >= 0.0, 1.0, 0.0))
        ok = ok * jnp.where(row8 < 4, jnp.where(j < 8.0, 1.0, 0.0), jnp.where(j < 4.0, 1.0, 0.0))
        r = row8f - j
        routes.append(jnp.where(ok > 0.5, jnp.where(r < 0.0, r + 8.0, r), 99.0))
    even8 = (lane8 & 1) == 0
    for g in range(4):
        rel_local[g], route[g] = rels[g], routes[g]
        own.rel[g], own.bnd[g] = full[g], edges[g]
        rim.rel[g], rim.bnd[g] = rim_full[g], rim_edges[g]
    rel_local[4] = jnp.where(even, rels[4], rels[5])
    route[4] = jnp.where(even8, routes[4], routes[5])
    own.rel[4] = jnp.where(even, full[4], full[5])
    own.bnd[4] = jnp.where(even, edges[4], edges[5])
    rim.rel[4] = jnp.where(even, rim_full[4], rim_full[5])
    rim.bnd[4] = jnp.where(even, rim_edges[4], rim_edges[5])
    for st, e in ((own, edges), (rim, rim_edges)):
        st.bx = jnp.where(x_first, e[4], jnp.where(x_last, e[5], 0.0))
        st.by = (jnp.where(y_first, e[2], 0.0), jnp.where(y_last, e[3], 0.0))

    def fill_way(way):
        for slot in range(N_X):
            for m in range(6):
                recv[slot, way, m] = jnp.zeros((8, LN), F32)

    def fill_blocks(by):
        at = MINE + 16 * by
        link_w[at : at + 16] = jnp.ones((16, LN), F32)
        share_w[at : at + 16] = jnp.zeros((16, LN), F32)

    for way in range(2):
        pl.when(jnp.logical_not(has(2 * way - 1)))(functools.partial(fill_way, way))
    for by in (1, -1, 2, -2):
        pl.when(jnp.logical_not(has(by)))(functools.partial(fill_blocks, by))

    def plane_of(ref):
        return lambda z, h: ref[:, z * 256 + h * LN : z * 256 + (h + 1) * LN]

    def from_input(ref, store=None):
        def produce(zg, i):
            at = pl.multiple_of((zg * 8 + i) * 256, 256)
            v0, v1 = ref[:, pl.ds(at, LN)], ref[:, pl.ds(at + LN, LN)]
            if store is not None:
                store[zg * 8 + i + 1, :, chunk(0)] = v0
                store[zg * 8 + i + 1, :, chunk(1)] = v1
            return v0, v1

        return produce

    loads[0].wait()
    faces_of(from_input(own.mu_v), own_mu, plane_of(own.mu_v))
    sources(own_mu, src_w)
    pl.semaphore_wait(barrier, greeted)
    send_faces(src_w, X_MU)
    loads[2].wait()
    faces_of(from_input(own.u0_v, own.u), own.faces, plane_of(own.u0_v))
    sources(own.faces, src_f)
    send_faces(src_f, X_U0)
    local_ghosts(src_f, near_local.at[0])
    start(ghost_copies(0))
    loads[3].wait()
    start(field_copies(0))
    start(field_copies(2))

    local_ghosts(src_w, mu_f)
    for st in both:
        for ref in (st.u, st.w):
            ref[0] = jnp.zeros((BLK, 256), F32)
            ref[BE + 1] = jnp.zeros((BLK, 256), F32)
        st.cz[0] = jnp.zeros((BLK, 256), F32)
        st.cz[BE] = jnp.zeros((BLK, 256), F32)

    def mean(a, b):
        return 2.0 * a * b / (a + b)

    def inner_couplings(st):
        def body(z):
            at = pl.multiple_of(z * 256, 256)
            m0, m1 = st.mu_v[:, pl.ds(at, LN)], st.mu_v[:, pl.ds(at + LN, LN)]
            y0, y1 = lower_y(m0, m1)
            st.cx[z, :, chunk(0)] = jnp.where(x_first, 0.0, mean(m0, turn(m0, 1)))
            st.cx[z, :, chunk(1)] = jnp.where(x_first, 0.0, mean(m1, turn(m1, 1)))
            st.cy[z, :, chunk(0)] = jnp.where(y_first, 0.0, mean(m0, y0))
            st.cy[z, :, chunk(1)] = mean(m1, y1)

        def across_z(z):
            at = pl.multiple_of(z * 256, 256)
            st.cz[z + 1] = mean(st.mu_v[:, pl.ds(at, 256)], st.mu_v[:, pl.ds(at + 256, 256)])

        steps(BE, body)
        steps(BE - 1, across_z)

    inner_couplings(own)

    def around(st, z):
        cx0, cx1 = st.cx[z, :, chunk(0)], st.cx[z, :, chunk(1)]
        cy0, cy1 = st.cy[z, :, chunk(0)], st.cy[z, :, chunk(1)]
        uy0, uy1 = upper_y(cy0, cy1)
        uy1 = jnp.where(y_last, 0.0, uy1)
        lo = (st.cz[z, :, chunk(0)], st.cz[z, :, chunk(1)])
        up = (st.cz[z + 1, :, chunk(0)], st.cz[z + 1, :, chunk(1)])
        return (
            (lo[0], up[0], cy0, uy0, cx0, turn(cx0, -1)),
            (lo[1], up[1], cy1, uy1, cx1, turn(cx1, -1)),
        )

    def beside(ref, z):
        v0, v1 = ref[z + 1, :, chunk(0)], ref[z + 1, :, chunk(1)]
        l0, l1 = lower_y(v0, v1)
        p0, p1 = upper_y(v0, v1)
        return (v0, v1), (
            (ref[z, :, chunk(0)], ref[z + 2, :, chunk(0)], l0, p0, turn(v0, 1), turn(v0, -1)),
            (ref[z, :, chunk(1)], ref[z + 2, :, chunk(1)], l1, p1, turn(v1, 1), turn(v1, -1)),
        )

    def first_terms(st):
        def body(z, acc):
            c = around(st, z)
            _, n = beside(st.u, z)
            for h in range(2):
                at = pl.multiple_of(z * 256 + h * LN, LN)
                r = st.rs_v[:, pl.ds(at, LN)]
                d = c[h][0]
                t = r + c[h][0] * n[h][0]
                for f in range(1, 6):
                    d = d + c[h][f]
                    t = t + c[h][f] * n[h][f]
                st.dint[z, :, chunk(h)] = d
                st.t0[z, :, chunk(h)] = t
                acc = acc + r
            return acc

        return steps(BE, body, zero)

    acc = first_terms(own)
    rsum[...] = jnp.broadcast_to(jnp.sum(acc, axis=1, keepdims=True), (BLK, LN))

    add_remote(X_MU, mu_f, own.ghost)
    for k in range(12):
        m = own_mu[k]
        g = jnp.where(own.bnd[GROUP[k]] > 0.5, m, own.ghost[k])
        own.cface[k] = mean(m, g)
    add_remote(X_U0, near_local.at[0], own.ghost)

    def add_first_z(st):
        for k in range(12):
            pface[k] = st.cface[k] * st.ghost[k]
        for h in range(2):
            st.dint[0, :, chunk(h)] += st.cface[h]
            st.dint[BE - 1, :, chunk(h)] += st.cface[2 + h]
            st.t0[0, :, chunk(h)] += pface[h]
            st.t0[BE - 1, :, chunk(h)] += pface[2 + h]

    y_face = (y_first, y_last)

    def sweep_first(st):
        def produce(zg, i):
            z = zg * 8 + i
            vs = []
            for h in range(2):
                d = st.dint[z, :, chunk(h)]
                t = st.t0[z, :, chunk(h)]
                d = d + jnp.where(x_face, spread_x(st.cface, zg, i, h), 0.0)
                d = d + jnp.where(y_face[h], spread_y(st.cface, zg, i, h), 0.0)
                t = t + jnp.where(x_face, spread_x(pface, zg, i, h), 0.0)
                t = t + jnp.where(y_face[h], spread_y(pface, zg, i, h), 0.0)
                q = RELAX_FINE / d
                st.inv[z, :, chunk(h)] = q
                v = (1.0 - RELAX_FINE) * st.u[z + 1, :, chunk(h)] + q * t
                st.u[z + 1, :, chunk(h)] = v
                vs.append(v)
            return vs

        return produce

    def each_plane(produce):
        for zg in range(2):
            steps(8, lambda i, zg=zg: (produce(zg, i), None)[1])

    def plane_u(ref):
        return lambda z, h: ref[z + 1, :, chunk(h)]

    add_first_z(own)
    faces_of(sweep_first(own), own.faces, plane_u(own.u))
    sources(own.faces, src_f)
    send_faces(src_f, X_U1)
    start(field_copies(1))

    def coefficients(st):
        for h in range(2):
            st.gz[0, :, chunk(h)] = st.cface[h] * st.inv[0, :, chunk(h)]
            st.gz[1, :, chunk(h)] = st.cface[2 + h] * st.inv[BE - 1, :, chunk(h)]

        def produce(zg, i):
            z = zg * 8 + i
            c = around(st, z)
            for h in range(2):
                q = st.inv[z, :, chunk(h)]
                for f in range(6):
                    st.coef[f, z, :, chunk(h)] = c[h][f] * q
                at = pl.multiple_of(z * 256 + h * LN, LN)
                st.rhs[z, :, chunk(h)] = st.rs_v[:, pl.ds(at, LN)] * q
                fx = jnp.where(x_face, spread_x(st.cface, zg, i, h), 0.0) * q
                fy = jnp.where(y_face[h], spread_y(st.cface, zg, i, h), 0.0) * q
                st.gx[z, :, chunk(h)] = fx
                st.gy[z, :, chunk(h)] = fy
                st.w[z + 1, :, chunk(h)] = 1.0 - fx * st.bx - fy * st.by[h]

        each_plane(produce)
        for h in range(2):
            st.w[1, :, chunk(h)] -= st.gz[0, :, chunk(h)] * st.bnd[0]
            st.w[BE, :, chunk(h)] -= st.gz[1, :, chunk(h)] * st.bnd[1]

    def inner_sweep(st, ref, base_ref, with_rhs):
        def body(z):
            v, n = beside(ref, z)
            for h in range(2):
                b = (1.0 - RELAX_FINE) * v[h]
                if with_rhs:
                    b = b + st.rhs[z, :, chunk(h)]
                for f in range(6):
                    b = b + st.coef[f, z, :, chunk(h)] * n[h][f]
                base_ref[z, :, chunk(h)] = b

        steps(BE, body)

    def add_z(st, base_ref):
        for h in range(2):
            base_ref[0, :, chunk(h)] += st.gz[0, :, chunk(h)] * st.ghost[h]
            base_ref[BE - 1, :, chunk(h)] += st.gz[1, :, chunk(h)] * st.ghost[2 + h]

    def outer_sweep(st, base_ref, ref, fix=None):
        add_z(st, base_ref)

        def produce(zg, i):
            z = zg * 8 + i
            vs = []
            for h in range(2):
                v = base_ref[z, :, chunk(h)]
                if fix is not None:
                    v = v + fix
                v = v + st.gx[z, :, chunk(h)] * spread_x(st.ghost, zg, i, h)
                v = v + st.gy[z, :, chunk(h)] * spread_y(st.ghost, zg, i, h)
                ref[z + 1, :, chunk(h)] = v
                vs.append(v)
            return vs

        return produce

    local_ghosts(src_f, near_local.at[1])
    coefficients(own)
    inner_sweep(own, own.u, own.base, True)
    start(ghost_copies(1))
    start(coupling_copies())

    def face_sums(value):
        sums = []
        for f in range(4):
            s = value(2 * f) + value(2 * f + 1)
            sums.append(jnp.sum(s, axis=1, keepdims=True))
        s = value(8) + value(9) + value(10) + value(11)
        sums.append(jnp.sum(jnp.where(even, s, 0.0), axis=1, keepdims=True))
        sums.append(jnp.sum(jnp.where(even, 0.0, s), axis=1, keepdims=True))
        return sums

    links = face_sums(lambda k: own.cface[k])
    tile = zero
    link_total = links[0]
    for f in range(6):
        tile = jnp.where(lane == f, links[f], tile)
        if f:
            link_total = link_total + links[f]
    link_w[MINE : MINE + 16] = tile

    def spread_blocks(ref, a, b):
        mine = ref.at[pl.ds(MINE, 16)]
        return [
            (remote(mine, ref.at[pl.ds(MINE - 16 * by, 16)], a.at[i], b.at[i], dev(by)), by)
            for i, by in enumerate((1, -1, 2, -2))
        ]

    link_copies = spread_blocks(link_w, l_send, l_recv)
    start(link_copies)


    add_remote(X_U1, near_local.at[1], own.ghost)
    faces_of(outer_sweep(own, own.base, own.u), own.faces, plane_u(own.u))
    sources(own.faces, src_f)
    send_faces(src_f, X_U2)
    local_ghosts(src_f, near_local.at[2])
    start(ghost_copies(2))

    sums = face_sums(lambda k: own.cface[k] * own.faces[k])
    left = rsum[:, 0:1]
    group_left = left
    tile = zero
    for f in range(6):
        tile = jnp.where(lane == f, sums[f], tile)
        left = left - sums[f]
        group_left = group_left - sums[f] * edges[f][:, 0:1]
    share_w[MINE : MINE + 16] = jnp.where(lane == 6, left, tile)
    share_copies = spread_blocks(share_w, s_send, s_recv)
    start(share_copies)
    total[0] = jnp.where(
        lane8 < 64,
        jnp.sum(group_left, axis=0, keepdims=True),
        jnp.sum(link_total, axis=0, keepdims=True),
    )
    total_copies = [
        (remote(total.at[0], total.at[i], a_send.at[i], a_recv.at[i], in_group(i)), None)
        for i in range(1, n_sub)
    ]
    start(total_copies)

    inner_sweep(own, own.u, own.base, True)
    arrive(field_copies(0))
    inner_couplings(rim)
    arrive(field_copies(1) + field_copies(2))
    each_plane(from_input(rim.u0_v, rim.u))
    first_terms(rim)
    arrive(coupling_copies())
    rim_ghosts(0)
    add_first_z(rim)
    each_plane(sweep_first(rim))
    coefficients(rim)
    inner_sweep(rim, rim.u, rim.base, True)
    rim_ghosts(1)
    each_plane(outer_sweep(rim, rim.base, rim.u))
    inner_sweep(rim, rim.u, rim.base, True)

    arrive(link_copies)
    iw = lax.broadcasted_iota(I32, (WIN, WIN), 0)
    lw = lax.broadcasted_iota(I32, (WIN, WIN), 1)
    lwf = lw.astype(F32)
    diagonal = link_w[:, 0:1]
    for f in range(1, 6):
        diagonal = diagonal + link_w[:, f : f + 1]
    gain = RELAX_COARSE / diagonal
    ident = jnp.where(iw == lw, 1.0, 0.0)
    hot = [jnp.where(col[0:WIN, f : f + 1] == lwf, 1.0, 0.0) for f in range(6)]
    gmat = link_w[:, 0:1] * hot[0]
    for f in range(1, 6):
        gmat = gmat + link_w[:, f : f + 1] * hot[f]
    gmat = gmat * gain + (1.0 - RELAX_COARSE) * ident

    def product(a, b):
        return lax.dot_general(
            a,
            b,
            (((1,), (0,)), ((), ())),
            precision=lax.Precision.HIGHEST,
            preferred_element_type=F32,
        )

    ymat = ident + gmat
    ymat = ident + product(ymat, gmat)
    ymat = ident + product(ymat, gmat)
    scale = jnp.sum(ident * gain, axis=0, keepdims=True)

    def pick(m):
        return [m[MINE : MINE + 16], m[MINE - 8 : MINE], m[MINE + 16 : MINE + 24]]

    picks = jnp.concatenate(sum([pick(m) for m in [ident] + hot], []), axis=0)
    qmat[...] = product(picks, ymat) * scale

    arrive(total_copies)
    part = total[0]
    for i in range(1, n_sub):
        part = part + total[i]
    group_total[0] = part
    group_copies = [
        (remote(group_total.at[0], group_total.at[i], b_send.at[i], b_recv.at[i], across(i)), None)
        for i in range(1, n_grp)
    ]
    start(group_copies)

    def from_w(st):
        def produce(zg, i):
            z = zg * 8 + i
            return st.w[z + 1, :, chunk(0)], st.w[z + 1, :, chunk(1)]

        return produce

    for st in both:
        faces_of(from_w(st), st.wfaces, plane_u(st.w))
        sources(st.wfaces, src_w, st is rim)
        inner_sweep(st, st.w, st.base_w, False)
    for st in both:
        all_ghosts(src_w, st)
        each_plane(outer_sweep(st, st.base_w, st.w))

    arrive(share_copies)
    acc = ident * share_w[:, 6:7]
    iwf = iw.astype(F32)
    for f in range(6):
        acc = acc + jnp.where(nb[f : f + 1, 0:WIN] == iwf, share_w[:, (f ^ 1) : (f ^ 1) + 1], 0.0)
    source_row = jnp.sum(acc, axis=0, keepdims=True)
    fixed = jnp.sum(qmat[...] * source_row, axis=1, keepdims=True)
    for n, st in enumerate(both):
        fix = fixed[16 * n : 16 * n + 16]
        st.corr[0] = jnp.broadcast_to(fix, (BLK, LN))
        gains = []
        for f in range(6):
            at = 32 * (f + 1) + 16 * n
            gains.append(jnp.broadcast_to(fixed[at : at + 16] - fix, (BLK, LN)))
        for f in range(4):
            st.corr[1 + f] = gains[f]
        st.corr[5] = jnp.where(even, gains[4], gains[5])

    def third_sweep(st):
        for k in range(12):
            st.ghost[k] += st.corr[1 + GROUP[k]]
        produce = outer_sweep(st, st.base, st.u, st.corr[0])
        faces_of(produce, st.faces, plane_u(st.u))
        sources(st.faces, src_f, st is rim)

    add_remote(X_U2, near_local.at[2], own.ghost)
    third_sweep(own)
    inner_sweep(own, own.u, own.base, True)
    rim_ghosts(2)
    third_sweep(rim)
    inner_sweep(rim, rim.u, rim.base, True)
    for st in both:
        all_ghosts(src_f, st)

    arrive(group_copies)
    part = group_total[0]
    for i in range(1, n_grp):
        part = part + group_total[i]
    level = part[0:1, 0:1] / part[0:1, 64:65]
    level = jnp.broadcast_to(level, (BLK, LN))

    def last_sweep(st):
        add_z(st, st.base)

        def produce(zg, i):
            z = zg * 8 + i
            for h in range(2):
                v = st.base[z, :, chunk(h)] + level * st.w[z + 1, :, chunk(h)]
                v = v + st.gx[z, :, chunk(h)] * spread_x(st.ghost, zg, i, h)
                v = v + st.gy[z, :, chunk(h)] * spread_y(st.ghost, zg, i, h)
                if st is rim:
                    window[2 * z + h, 0:8, :] = v[0:8]
                    window[2 * z + h, 24:32, :] = v[8:16]
                else:
                    window[2 * z + h, 8:24, :] = v

        each_plane(produce)

    for st in both:
        last_sweep(st)

    loads[4].wait()
    owners = own_v[...]
    starts = jnp.sum(jnp.where(owners < me, 1.0, 0.0)).astype(I32)
    count = jnp.sum(jnp.where(owners == me, 1.0, 0.0)).astype(I32)
    at = jnp.clip(starts - BLK * me + 8, 4, 12)
    row24 = lax.broadcasted_iota(I32, (CAP, LN), 0)
    live = row24 < count

    def emit(z):
        for h in range(2):
            lanes = pl.ds(pl.multiple_of(z * 256 + h * LN, LN), LN)
            out[:, lanes] = jnp.where(live, window[2 * z + h, pl.ds(at, CAP), :], 0.0)

    steps(BE, emit)

    for slot in range(N_X):
        finish(face_copies(slot))
    for slot in range(3):
        finish(ghost_copies(slot) + field_copies(slot))
    finish(coupling_copies() + link_copies + share_copies + total_copies + group_copies)


def local(potential, right_side, permeability, new_owner, neighbours):
    n_grp, n_sub = lax.axis_size("grp"), lax.axis_size("sub")
    nblk = new_owner.shape[0]
    vmem = pltpu.VMEM
    plane = (BLK, 256)
    dma = pltpu.SemaphoreType.DMA
    faces = (12, BLK, LN)
    scratch = [
        vmem((2, BLK, 4096), F32),
        vmem((2, BLK, 4096), F32),
        vmem((2, BLK, 4096), F32),
        vmem((nblk // LN, LN), I32),
        vmem((6, nblk), I32),
        vmem((2, BE + 2, *plane), F32),
        vmem((2, BE + 2, *plane), F32),
        vmem((2, BE, *plane), F32),
        vmem((2, BE, *plane), F32),
        vmem((2, BE + 1, *plane), F32),
        vmem((2, BE, *plane), F32),
        vmem((2, BE, *plane), F32),
        vmem((2, BE, *plane), F32),
        vmem((2, 6, BE, *plane), F32),
        vmem((2, BE, *plane), F32),
        vmem((2, BE, *plane), F32),
        vmem((2, BE, *plane), F32),
        vmem((2, 2, *plane), F32),
        vmem((2, BE, *plane), F32),
        vmem((2, BE, *plane), F32),
        vmem((2, *faces), F32),
        vmem((2, *faces), F32),
        vmem((2, *faces), F32),
        vmem((2, *faces), F32),
        vmem((2, 5, BLK, LN), F32),
        vmem((2, 5, BLK, LN), F32),
        vmem((2, 6, BLK, LN), F32),
        vmem(faces, F32),
        vmem(faces, F32),
        vmem(faces, F32),
        vmem((12, 48, LN), F32),
        vmem((12, 48, LN), F32),
        vmem((3, *faces), F32),
        vmem((3, *faces), F32),
        vmem((3, 12, 8, LN), F32),
        vmem((5, BLK, LN), F32),
        vmem((5, 8, LN), F32),
        vmem((LN, 8), F32),
        vmem((224, WIN), F32),
        vmem((WIN, LN), F32),
        vmem((WIN, LN), F32),
        vmem((BLK, LN), F32),
        vmem((N_X, 2, 6, 8, LN), F32),
        vmem((N_X, 2, 6, 8, LN), F32),
        vmem((n_sub, 8, LN), F32),
        vmem((n_grp, 8, LN), F32),
        vmem((32, 40, LN), F32),
        dma((5,)),
        dma((N_X, 2)),
        dma((N_X, 2)),
        dma((4,)),
        dma((4,)),
        dma((4,)),
        dma((4,)),
        dma((n_sub,)),
        dma((n_sub,)),
        dma((n_grp,)),
        dma((n_grp,)),
        dma((3, 2)),
        dma((3, 2)),
        dma((3, 2)),
        dma((3, 2)),
        dma((2,)),
        dma((2,)),
    ]
    return pl.pallas_call(
        functools.partial(kernel, n_grp, n_sub, nblk),
        out_shape=jax.ShapeDtypeStruct((CAP, 4096), F32),
        in_specs=[pl.BlockSpec(memory_space=pl.ANY)] * 5,
        out_specs=pl.BlockSpec(memory_space=pltpu.VMEM),
        scratch_shapes=scratch,
        compiler_params=pltpu.CompilerParams(
            collective_id=0, has_side_effects=True, vmem_limit_bytes=60 * 1024 * 1024
        ),
        cost_estimate=pl.CostEstimate(
            flops=8_000_000, bytes_accessed=1_200_000, transcendentals=0
        ),
        name="cycle",
    )(potential, right_side, permeability, new_owner.reshape(nblk // LN, LN), neighbours)


def solution(mesh):
    in_specs = (P(("grp", "sub"), None), P(("grp", "sub"), None), P(("grp", "sub"), None), P(), P())
    out_specs = P(("grp", "sub"), None)
    return jax.shard_map(local, mesh=mesh, in_specs=in_specs, out_specs=out_specs, check_vma=False)
```

```python
import functools
import types

import jax
import jax.numpy as jnp
from jax import lax
from jax.experimental import pallas as pl
from jax.experimental.pallas import tpu as pltpu
from jax.sharding import PartitionSpec as P

BE = 16
BLK = 16
CAP = 24
LN = 128
RELAX_FINE = 0.8
RELAX_COARSE = 0.7
MESH = pl.DeviceIdType.MESH
F32 = jnp.float32
I32 = jnp.int32
GROUP = (0, 0, 1, 1, 2, 2, 3, 3, 4, 4, 4, 4)
SOURCE = (2, 3, 0, 1, 6, 7, 4, 5)
X_MU, X_U0, X_U1, X_U2 = range(4)
N_X = 4
WIN = 80
MINE = 32


def chunk(h):
    return slice(h * LN, (h + 1) * LN)


def steps(n, body, init=None):
    if init is None:
        lax.fori_loop(0, n, lambda i, _: (body(i), 0)[1], 0, unroll=n)
        return None
    return lax.fori_loop(0, n, body, init, unroll=n)


def kernel(
    n_grp, n_sub, nblk,
    pot, rs, mu, owner, neigh, out,
    mu_s, u0_s, rs_s, own_v, nb_v,
    u_s, w_s, cx_s, cy_s, cz_s, dint_s, t0_s, inv_s, coef_s, rhs_s, gx_s, gy_s, gz_s, base_s, base_w_s,
    faces_s, wfaces_s, ghost_s, cface_s, rel_s, bnd_s, corr_s,
    pface, mu_f, own_mu, src_f, src_w, near_local, near_far, keep,
    rel_local, route, col, qmat, link_w, share_w, rsum,
    send, recv, total, group_total, window,
    in_sem, x_send, x_recv, l_send, l_recv, s_send, s_recv,
    a_send, a_recv, b_send, b_recv, k_send, k_recv, g_send, g_recv, c_send, c_recv,
):
    def state(k):
        return types.SimpleNamespace(
            mu_v=mu_s.at[k], u0_v=u0_s.at[k], rs_v=rs_s.at[k], u=u_s.at[k], w=w_s.at[k],
            cx=cx_s.at[k], cy=cy_s.at[k], cz=cz_s.at[k], dint=dint_s.at[k], t0=t0_s.at[k],
            inv=inv_s.at[k], coef=coef_s.at[k], rhs=rhs_s.at[k], gx=gx_s.at[k], gy=gy_s.at[k],
            gz=gz_s.at[k], base=base_s.at[k], base_w=base_w_s.at[k], faces=faces_s.at[k],
            wfaces=wfaces_s.at[k], ghost=ghost_s.at[k], cface=cface_s.at[k], rel=rel_s.at[k],
            bnd=bnd_s.at[k], corr=corr_s.at[k],
        )

    own, rim = state(0), state(1)
    both = (own, rim)
    grp, sub = lax.axis_index("grp"), lax.axis_index("sub")
    devices = n_grp * n_sub
    me = grp * n_sub + sub

    def dev(by):
        other = lax.rem(me + by + devices, devices)
        return (lax.div(other, n_sub), lax.rem(other, n_sub))

    def in_group(by):
        return (grp, lax.rem(sub + by + n_sub, n_sub))

    def across(by):
        return (lax.rem(grp + by + n_grp, n_grp), sub)

    def has(by):
        return (me + by >= 0) & (me + by < devices)

    barrier = pltpu.get_barrier_semaphore()

    def greet(to):
        pl.semaphore_signal(barrier, inc=1, device_id=to, device_id_type=MESH)

    greeted = n_sub - 1 + n_grp - 1
    for by in (1, -1, 2, -2):
        pl.when(has(by))(functools.partial(greet, dev(by)))
        greeted = greeted + has(by).astype(I32)
    for by in range(1, n_sub):
        greet(in_group(by))
    for by in range(1, n_grp):
        greet(across(by))

    loads = [
        pltpu.make_async_copy(a, b, in_sem.at[i])
        for i, (a, b) in enumerate(
            ((mu, own.mu_v), (neigh, nb_v), (pot, own.u0_v), (rs, own.rs_v), (owner, own_v))
        )
    ]
    for copy in loads:
        copy.start()

    lane = lax.broadcasted_iota(I32, (BLK, LN), 1)
    xpos = lane & 15
    yrow = lane >> 4
    row = lax.broadcasted_iota(I32, (BLK, LN), 0)
    lane8 = lax.broadcasted_iota(I32, (8, LN), 1)
    row8 = lax.broadcasted_iota(I32, (8, LN), 0)
    x_first, x_last = xpos == 0, xpos == BE - 1
    x_face = x_first | x_last
    y_first, y_last = lane < BE, lane >= LN - BE
    even = (lane & 1) == 0
    zero = jnp.zeros((BLK, LN), F32)

    def turn(v, by):
        if isinstance(by, int):
            by = by % LN
            return v if by == 0 else pltpu.roll(v, by, 1)
        return pltpu.roll(v, by & (LN - 1), 1)

    def lower_y(v0, v1):
        a, b = turn(v0, BE), turn(v1, BE)
        return a, jnp.where(y_first, a, b)

    def upper_y(v0, v1):
        a, b = turn(v0, -BE), turn(v1, -BE)
        return jnp.where(y_last, b, a), b

    def remote(src, dst, a, b, to):
        return pltpu.make_async_remote_copy(
            src_ref=src, dst_ref=dst, send_sem=a, recv_sem=b, device_id=to, device_id_type=MESH
        )

    def faces_of(produce, faces_ref, plane):
        for zg in range(2):
            def body(i, carry, zg=zg):
                x0, x1, y2, y3 = carry
                v0, v1 = produce(zg, i)
                here = (xpos == 2 * i) | (xpos == ((2 * i + 15) & 15))
                x0 = jnp.where(here, turn(v0, 2 * i), x0)
                x1 = jnp.where(here, turn(v1, 2 * i), x1)
                line = yrow == i
                y2 = jnp.where(line, turn(v0, BE * i), y2)
                y3 = jnp.where(line, turn(v1, BE * i + BE), y3)
                return x0, x1, y2, y3

            x0, x1, y2, y3 = steps(8, body, (zero, zero, zero, zero))
            faces_ref[8 + 2 * zg] = x0
            faces_ref[9 + 2 * zg] = x1
            faces_ref[4 + zg] = y2
            faces_ref[6 + zg] = y3
        for h in range(2):
            faces_ref[h] = plane(0, h)
            faces_ref[2 + h] = plane(BE - 1, h)

    def sources(faces_ref, src_ref, is_rim=False):
        for k in range(12):
            if k < 8:
                v = faces_ref[SOURCE[k]]
            else:
                x = faces_ref[k]
                v = jnp.where(even, turn(x, -15), turn(x, 15))
            if is_rim:
                src_ref[k, 8:16, :] = v[0:8]
                src_ref[k, 32:40, :] = v[8:16]
            else:
                src_ref[k, 16:32, :] = v

    def send_faces(src_ref, slot):
        for m in range(6):
            pair = []
            for k in (2 * m, 2 * m + 1):
                edge = jnp.where(row8 < 4, src_ref[k, 16:24, :], src_ref[k, 24:32, :])
                way = route[GROUP[k]]
                d = jnp.zeros((8, LN), F32)
                for r in (4,) if k < 4 else range(1, 8):
                    d = jnp.where(way == r, pltpu.roll(edge, r, 0), d)
                pair.append(d)
                if slot:
                    keep[slot - 1, k] = d
            d0, d1 = pair
            send[slot, 0, m] = jnp.where(row8 < 4, d0, pltpu.roll(d1, 4, 0))
            send[slot, 1, m] = jnp.where(row8 < 4, pltpu.roll(d0, 4, 0), d1)
        start(face_copies(slot))

    def face_copies(slot):
        return [
            (
                remote(
                    send.at[slot, way],
                    recv.at[slot, way],
                    x_send.at[slot, way],
                    x_recv.at[slot, way],
                    dev(1 - 2 * way),
                ),
                1 - 2 * way,
            )
            for way in range(2)
        ]

    def local_ghosts(src_ref, ghost_ref):
        for k in range(12):
            r = rel_local[GROUP[k]]
            g = zero
            for by in (-4, 4) if k < 4 else range(-4, 5):
                g = jnp.where(r == by, src_ref[k, 16 + by : 32 + by, :], g)
            ghost_ref[k] = g

    def all_ghosts(src_ref, st):
        for k in range(12):
            r = st.rel[GROUP[k]]
            tops = (8, 32) if st is rim else (16, 24)
            for t in range(2):
                g = jnp.zeros((8, LN), F32)
                rt = r[8 * t : 8 * t + 8]
                for by in (-4, 4) if k < 4 else range(-4, 5):
                    g = jnp.where(rt == by, src_ref[k, tops[t] + by : tops[t] + by + 8, :], g)
                st.ghost[k, 8 * t : 8 * t + 8, :] = g

    def add_remote(slot, near_ref, ghost_ref):
        arrive(face_copies(slot))
        for m in range(6):
            lo, hi = recv[slot, 0, m], recv[slot, 1, m]
            lo1, hi0 = pltpu.roll(lo, 4, 0), pltpu.roll(hi, 4, 0)
            a, b = 2 * m, 2 * m + 1
            ghost_ref[a, 0:8, :] = near_ref[a, 0:8, :] + jnp.where(row8 < 4, lo, 0.0)
            ghost_ref[b, 0:8, :] = near_ref[b, 0:8, :] + jnp.where(row8 < 4, lo1, 0.0)
            ghost_ref[a, 8:16, :] = near_ref[a, 8:16, :] + jnp.where(row8 < 4, 0.0, hi0)
            ghost_ref[b, 8:16, :] = near_ref[b, 8:16, :] + jnp.where(row8 < 4, 0.0, hi)

    def rows_both_ways(src, dst, a, b):
        return [
            (remote(src(8), dst(0), a.at[0], b.at[0], dev(1)), 1),
            (remote(src(0), dst(8), a.at[1], b.at[1], dev(-1)), -1),
        ]

    def field_copies(k):
        ref = (mu_s, u0_s, rs_s, u0_s)[k]
        lanes = {1: pl.ds(0, 2048), 3: pl.ds(2048, 2048)}.get(k, pl.ds(0, 4096))
        return rows_both_ways(
            lambda r: ref.at[0, pl.ds(r, 8), lanes],
            lambda r: ref.at[1, pl.ds(r, 8), lanes],
            k_send.at[k],
            k_recv.at[k],
        )

    def ghost_copies(slot):
        return rows_both_ways(
            lambda r: near_local.at[slot, :, pl.ds(r, 8)],
            lambda r: near_far.at[slot, :, pl.ds(r, 8)],
            g_send.at[slot],
            g_recv.at[slot],
        )

    def coupling_copies():
        return rows_both_ways(
            lambda r: cface_s.at[0, :, pl.ds(r, 8)],
            lambda r: cface_s.at[1, :, pl.ds(r, 8)],
            c_send,
            c_recv,
        )

    def start(copies):
        for copy, by in copies:
            if by is None:
                copy.start()
            else:
                pl.when(has(by))(copy.start)

    def arrive(copies):
        for copy, by in copies:
            if by is None:
                copy.wait_recv()
            else:
                pl.when(has(-by))(copy.wait_recv)

    def finish(copies):
        for copy, by in copies:
            if by is None:
                copy.wait_send()
            else:
                pl.when(has(by))(copy.wait_send)

    def rim_ghosts(slot):
        arrive(ghost_copies(slot))
        for k in range(12):
            d = keep[slot, k]
            rim.ghost[k, 0:8, :] = near_far[slot, k, 0:8, :] + jnp.where(row8 < 4, 0.0, d)
            rim.ghost[k, 8:16, :] = near_far[slot, k, 8:16, :] + jnp.where(row8 < 4, d, 0.0)

    def spread_x(faces_ref, zg, i, h):
        return turn(faces_ref[8 + 2 * zg + h], LN - 2 * i)

    def spread_y(faces_ref, zg, i, h):
        return turn(faces_ref[(4, 6)[h] + zg], LN - BE * i - (0, BE)[h])

    first = BLK * me - MINE
    loads[1].wait()
    low = lax.div(first + LN, LN) - 1
    shift = first - low * LN
    tiles = nblk // LN

    def table(k):
        at = pl.multiple_of(lax.rem(k + tiles, tiles) * LN, LN)
        rows6 = nb_v[:, pl.ds(at, LN)]
        return jnp.concatenate([rows6, jnp.full((2, LN), -1, I32)], axis=0)

    back = LN - shift
    ta, tb = turn(table(low), back), turn(table(low + 1), back)
    ids = first + lane8
    nb = jnp.where(lane8 < back, ta, tb)
    nb = jnp.where((nb >= 0) & (ids >= 0) & (ids < nblk), nb - first, -1000).astype(F32)
    nbt = nb.T
    col[...] = nbt

    def columns(f, lo, n):
        return jnp.broadcast_to(col[lo : lo + n, f : f + 1], (n, LN))

    rowf = row.astype(F32)
    row8f = row8.astype(F32)
    rim_row = jnp.where(row < 8, rowf + (MINE - 8.0), rowf + (MINE + 8.0))
    far = jnp.zeros((BLK, LN), F32) + 99.0
    rels, routes, edges, full, rim_full, rim_edges = [], [], [], [], [], []
    for f in range(6):
        to = columns(f, MINE, 16)
        step = to - float(MINE) - rowf
        near = (to >= float(MINE)) & (to < MINE + 16.0)
        rels.append(jnp.where(near, step, far))
        full.append(step)
        edges.append(jnp.where(to < 0.0, 1.0, 0.0))
        before, after = columns(f, MINE - 8, 8), columns(f, MINE + 16, 8)
        to = jnp.concatenate([before, after], axis=0)
        rim_full.append(to - rim_row)
        rim_edges.append(jnp.where(to < 0.0, 1.0, 0.0))
        to8 = jnp.where(row8 < 4, after, before)
        j = jnp.where(row8 < 4, to8 - (MINE + 8.0), to8 - float(MINE))
        ok = jnp.where(row8 < 4, jnp.where(j >= 4.0, 1.0, 0.0), jnp.where(j >= 0.0, 1.0, 0.0))
        ok = ok * jnp.where(row8 < 4, jnp.where(j < 8.0, 1.0, 0.0), jnp.where(j < 4.0, 1.0, 0.0))
        r = row8f - j
        routes.append(jnp.where(ok > 0.5, jnp.where(r < 0.0, r + 8.0, r), 99.0))
    even8 = (lane8 & 1) == 0
    for g in range(4):
        rel_local[g], route[g] = rels[g], routes[g]
        own.rel[g], own.bnd[g] = full[g], edges[g]
        rim.rel[g], rim.bnd[g] = rim_full[g], rim_edges[g]
    rel_local[4] = jnp.where(even, rels[4], rels[5])
    route[4] = jnp.where(even8, routes[4], routes[5])
    own.rel[4] = jnp.where(even, full[4], full[5])
    own.bnd[4] = jnp.where(even, edges[4], edges[5])
    rim.rel[4] = jnp.where(even, rim_full[4], rim_full[5])
    rim.bnd[4] = jnp.where(even, rim_edges[4], rim_edges[5])
    for st, e in ((own, edges), (rim, rim_edges)):
        st.bx = jnp.where(x_first, e[4], jnp.where(x_last, e[5], 0.0))
        st.by = (jnp.where(y_first, e[2], 0.0), jnp.where(y_last, e[3], 0.0))

    def fill_way(way):
        for slot in range(N_X):
            for m in range(6):
                recv[slot, way, m] = jnp.zeros((8, LN), F32)

    def fill_blocks(by):
        at = MINE + 16 * by
        link_w[at : at + 16] = jnp.ones((16, LN), F32)
        share_w[at : at + 16] = jnp.zeros((16, LN), F32)

    for way in range(2):
        pl.when(jnp.logical_not(has(2 * way - 1)))(functools.partial(fill_way, way))
    for by in (1, -1, 2, -2):
        pl.when(jnp.logical_not(has(by)))(functools.partial(fill_blocks, by))

    def plane_of(ref):
        return lambda z, h: ref[:, z * 256 + h * LN : z * 256 + (h + 1) * LN]

    def from_input(ref, store=None):
        def produce(zg, i):
            at = pl.multiple_of((zg * 8 + i) * 256, 256)
            v0, v1 = ref[:, pl.ds(at, LN)], ref[:, pl.ds(at + LN, LN)]
            if store is not None:
                store[zg * 8 + i + 1, :, chunk(0)] = v0
                store[zg * 8 + i + 1, :, chunk(1)] = v1
            return v0, v1

        return produce

    loads[0].wait()
    faces_of(from_input(own.mu_v), own_mu, plane_of(own.mu_v))
    sources(own_mu, src_w)
    pl.semaphore_wait(barrier, greeted)
    send_faces(src_w, X_MU)
    loads[2].wait()
    faces_of(from_input(own.u0_v, own.u), own.faces, plane_of(own.u0_v))
    sources(own.faces, src_f)
    send_faces(src_f, X_U0)
    local_ghosts(src_f, near_local.at[0])
    loads[3].wait()
    start(field_copies(0))
    start(field_copies(2))
    start(field_copies(3))

    local_ghosts(src_w, mu_f)
    for st in both:
        for ref in (st.u, st.w):
            ref[0] = jnp.zeros((BLK, 256), F32)
            ref[BE + 1] = jnp.zeros((BLK, 256), F32)
        st.cz[0] = jnp.zeros((BLK, 256), F32)
        st.cz[BE] = jnp.zeros((BLK, 256), F32)

    def mean(a, b):
        return 2.0 * a * b / (a + b)

    def inner_couplings(st):
        def body(z):
            at = pl.multiple_of(z * 256, 256)
            m0, m1 = st.mu_v[:, pl.ds(at, LN)], st.mu_v[:, pl.ds(at + LN, LN)]
            y0, y1 = lower_y(m0, m1)
            st.cx[z, :, chunk(0)] = jnp.where(x_first, 0.0, mean(m0, turn(m0, 1)))
            st.cx[z, :, chunk(1)] = jnp.where(x_first, 0.0, mean(m1, turn(m1, 1)))
            st.cy[z, :, chunk(0)] = jnp.where(y_first, 0.0, mean(m0, y0))
            st.cy[z, :, chunk(1)] = mean(m1, y1)

        def across_z(z):
            at = pl.multiple_of(z * 256, 256)
            st.cz[z + 1] = mean(st.mu_v[:, pl.ds(at, 256)], st.mu_v[:, pl.ds(at + 256, 256)])

        steps(BE, body)
        steps(BE - 1, across_z)

    inner_couplings(own)

    def around(st, z):
        cx0, cx1 = st.cx[z, :, chunk(0)], st.cx[z, :, chunk(1)]
        cy0, cy1 = st.cy[z, :, chunk(0)], st.cy[z, :, chunk(1)]
        uy0, uy1 = upper_y(cy0, cy1)
        uy1 = jnp.where(y_last, 0.0, uy1)
        lo = (st.cz[z, :, chunk(0)], st.cz[z, :, chunk(1)])
        up = (st.cz[z + 1, :, chunk(0)], st.cz[z + 1, :, chunk(1)])
        return (
            (lo[0], up[0], cy0, uy0, cx0, turn(cx0, -1)),
            (lo[1], up[1], cy1, uy1, cx1, turn(cx1, -1)),
        )

    def beside(ref, z):
        v0, v1 = ref[z + 1, :, chunk(0)], ref[z + 1, :, chunk(1)]
        l0, l1 = lower_y(v0, v1)
        p0, p1 = upper_y(v0, v1)
        return (v0, v1), (
            (ref[z, :, chunk(0)], ref[z + 2, :, chunk(0)], l0, p0, turn(v0, 1), turn(v0, -1)),
            (ref[z, :, chunk(1)], ref[z + 2, :, chunk(1)], l1, p1, turn(v1, 1), turn(v1, -1)),
        )

    def first_terms(st):
        def body(z, acc):
            c = around(st, z)
            _, n = beside(st.u, z)
            for h in range(2):
                at = pl.multiple_of(z * 256 + h * LN, LN)
                r = st.rs_v[:, pl.ds(at, LN)]
                d = c[h][0]
                t = r + c[h][0] * n[h][0]
                for f in range(1, 6):
                    d = d + c[h][f]
                    t = t + c[h][f] * n[h][f]
                st.dint[z, :, chunk(h)] = d
                st.t0[z, :, chunk(h)] = t
                acc = acc + r
            return acc

        return steps(BE, body, zero)

    acc = first_terms(own)
    rsum[...] = jnp.broadcast_to(jnp.sum(acc, axis=1, keepdims=True), (BLK, LN))

    add_remote(X_MU, mu_f, own.ghost)
    for k in range(12):
        m = own_mu[k]
        g = jnp.where(own.bnd[GROUP[k]] > 0.5, m, own.ghost[k])
        own.cface[k] = mean(m, g)
    add_remote(X_U0, near_local.at[0], own.ghost)

    def add_first_z(st):
        for k in range(12):
            pface[k] = st.cface[k] * st.ghost[k]
        for h in range(2):
            st.dint[0, :, chunk(h)] += st.cface[h]
            st.dint[BE - 1, :, chunk(h)] += st.cface[2 + h]
            st.t0[0, :, chunk(h)] += pface[h]
            st.t0[BE - 1, :, chunk(h)] += pface[2 + h]

    y_face = (y_first, y_last)

    def sweep_first(st):
        def produce(zg, i):
            z = zg * 8 + i
            vs = []
            for h in range(2):
                d = st.dint[z, :, chunk(h)]
                t = st.t0[z, :, chunk(h)]
                d = d + jnp.where(x_face, spread_x(st.cface, zg, i, h), 0.0)
                d = d + jnp.where(y_face[h], spread_y(st.cface, zg, i, h), 0.0)
                t = t + jnp.where(x_face, spread_x(pface, zg, i, h), 0.0)
                t = t + jnp.where(y_face[h], spread_y(pface, zg, i, h), 0.0)
                q = RELAX_FINE / d
                st.inv[z, :, chunk(h)] = q
                v = (1.0 - RELAX_FINE) * st.u[z + 1, :, chunk(h)] + q * t
                st.u[z + 1, :, chunk(h)] = v
                vs.append(v)
            return vs

        return produce

    def each_plane(produce):
        for zg in range(2):
            steps(8, lambda i, zg=zg: (produce(zg, i), None)[1])

    def plane_u(ref):
        return lambda z, h: ref[z + 1, :, chunk(h)]

    add_first_z(own)
    faces_of(sweep_first(own), own.faces, plane_u(own.u))
    sources(own.faces, src_f)
    send_faces(src_f, X_U1)
    start(field_copies(1))
    start(ghost_copies(0))

    def coefficients(st):
        for h in range(2):
            st.gz[0, :, chunk(h)] = st.cface[h] * st.inv[0, :, chunk(h)]
            st.gz[1, :, chunk(h)] = st.cface[2 + h] * st.inv[BE - 1, :, chunk(h)]

        def produce(zg, i):
            z = zg * 8 + i
            c = around(st, z)
            for h in range(2):
                q = st.inv[z, :, chunk(h)]
                for f in range(6):
                    st.coef[f, z, :, chunk(h)] = c[h][f] * q
                at = pl.multiple_of(z * 256 + h * LN, LN)
                st.rhs[z, :, chunk(h)] = st.rs_v[:, pl.ds(at, LN)] * q
                fx = jnp.where(x_face, spread_x(st.cface, zg, i, h), 0.0) * q
                fy = jnp.where(y_face[h], spread_y(st.cface, zg, i, h), 0.0) * q
                st.gx[z, :, chunk(h)] = fx
                st.gy[z, :, chunk(h)] = fy
                st.w[z + 1, :, chunk(h)] = 1.0 - fx * st.bx - fy * st.by[h]

        each_plane(produce)
        for h in range(2):
            st.w[1, :, chunk(h)] -= st.gz[0, :, chunk(h)] * st.bnd[0]
            st.w[BE, :, chunk(h)] -= st.gz[1, :, chunk(h)] * st.bnd[1]

    def inner_sweep(st, ref, base_ref, with_rhs):
        def body(z):
            v, n = beside(ref, z)
            for h in range(2):
                b = (1.0 - RELAX_FINE) * v[h]
                if with_rhs:
                    b = b + st.rhs[z, :, chunk(h)]
                for f in range(6):
                    b = b + st.coef[f, z, :, chunk(h)] * n[h][f]
                base_ref[z, :, chunk(h)] = b

        steps(BE, body)

    def add_z(st, base_ref):
        for h in range(2):
            base_ref[0, :, chunk(h)] += st.gz[0, :, chunk(h)] * st.ghost[h]
            base_ref[BE - 1, :, chunk(h)] += st.gz[1, :, chunk(h)] * st.ghost[2 + h]

    def outer_sweep(st, base_ref, ref, fix=None):
        add_z(st, base_ref)

        def produce(zg, i):
            z = zg * 8 + i
            vs = []
            for h in range(2):
                v = base_ref[z, :, chunk(h)]
                if fix is not None:
                    v = v + fix
                v = v + st.gx[z, :, chunk(h)] * spread_x(st.ghost, zg, i, h)
                v = v + st.gy[z, :, chunk(h)] * spread_y(st.ghost, zg, i, h)
                ref[z + 1, :, chunk(h)] = v
                vs.append(v)
            return vs

        return produce

    local_ghosts(src_f, near_local.at[1])
    coefficients(own)
    inner_sweep(own, own.u, own.base, True)
    start(ghost_copies(1))
    start(coupling_copies())

    def face_sums(value):
        sums = []
        for f in range(4):
            s = value(2 * f) + value(2 * f + 1)
            sums.append(jnp.sum(s, axis=1, keepdims=True))
        s = value(8) + value(9) + value(10) + value(11)
        sums.append(jnp.sum(jnp.where(even, s, 0.0), axis=1, keepdims=True))
        sums.append(jnp.sum(jnp.where(even, 0.0, s), axis=1, keepdims=True))
        return sums

    links = face_sums(lambda k: own.cface[k])
    tile = zero
    link_total = links[0]
    for f in range(6):
        tile = jnp.where(lane == f, links[f], tile)
        if f:
            link_total = link_total + links[f]
    link_w[MINE : MINE + 16] = tile

    def spread_blocks(ref, a, b):
        mine = ref.at[pl.ds(MINE, 16)]
        return [
            (remote(mine, ref.at[pl.ds(MINE - 16 * by, 16)], a.at[i], b.at[i], dev(by)), by)
            for i, by in enumerate((1, -1, 2, -2))
        ]

    link_copies = spread_blocks(link_w, l_send, l_recv)
    start(link_copies)


    add_remote(X_U1, near_local.at[1], own.ghost)
    faces_of(outer_sweep(own, own.base, own.u), own.faces, plane_u(own.u))
    sums = face_sums(lambda k: own.cface[k] * own.faces[k])
    left = rsum[:, 0:1]
    group_left = left
    tile = zero
    for f in range(6):
        tile = jnp.where(lane == f, sums[f], tile)
        left = left - sums[f]
        group_left = group_left - sums[f] * edges[f][:, 0:1]
    share_w[MINE : MINE + 16] = jnp.where(lane == 6, left, tile)
    total[0] = jnp.where(
        lane8 < 64,
        jnp.sum(group_left, axis=0, keepdims=True),
        jnp.sum(link_total, axis=0, keepdims=True),
    )
    total_copies = [
        (remote(total.at[0], total.at[i], a_send.at[i], a_recv.at[i], in_group(i)), None)
        for i in range(1, n_sub)
    ]
    start(total_copies)

    sources(own.faces, src_f)
    send_faces(src_f, X_U2)
    share_copies = spread_blocks(share_w, s_send, s_recv)
    start(share_copies)
    local_ghosts(src_f, near_local.at[2])
    start(ghost_copies(2))

    inner_sweep(own, own.u, own.base, True)
    arrive(field_copies(0))
    inner_couplings(rim)
    arrive(field_copies(1) + field_copies(2) + field_copies(3))
    each_plane(from_input(rim.u0_v, rim.u))
    first_terms(rim)
    arrive(coupling_copies())
    rim_ghosts(0)
    add_first_z(rim)
    each_plane(sweep_first(rim))
    coefficients(rim)
    inner_sweep(rim, rim.u, rim.base, True)
    rim_ghosts(1)
    each_plane(outer_sweep(rim, rim.base, rim.u))
    inner_sweep(rim, rim.u, rim.base, True)

    arrive(total_copies)
    part = total[0]
    for i in range(1, n_sub):
        part = part + total[i]
    group_total[0] = part
    group_copies = [
        (remote(group_total.at[0], group_total.at[i], b_send.at[i], b_recv.at[i], across(i)), None)
        for i in range(1, n_grp)
    ]
    start(group_copies)

    arrive(link_copies)
    iw = lax.broadcasted_iota(I32, (WIN, WIN), 0)
    lw = lax.broadcasted_iota(I32, (WIN, WIN), 1)
    lwf = lw.astype(F32)
    diagonal = link_w[:, 0:1]
    for f in range(1, 6):
        diagonal = diagonal + link_w[:, f : f + 1]
    gain = RELAX_COARSE / diagonal
    ident = jnp.where(iw == lw, 1.0, 0.0)
    hot = [jnp.where(col[0:WIN, f : f + 1] == lwf, 1.0, 0.0) for f in range(6)]
    gmat = link_w[:, 0:1] * hot[0]
    for f in range(1, 6):
        gmat = gmat + link_w[:, f : f + 1] * hot[f]
    gmat = gmat * gain + (1.0 - RELAX_COARSE) * ident

    def product(a, b):
        return lax.dot_general(
            a,
            b,
            (((1,), (0,)), ((), ())),
            precision=lax.Precision.HIGHEST,
            preferred_element_type=F32,
        )

    ymat = ident + gmat
    ymat = ident + product(ymat, gmat)
    ymat = ident + product(ymat, gmat)
    scale = jnp.sum(ident * gain, axis=0, keepdims=True)

    def pick(m):
        return [m[MINE : MINE + 16], m[MINE - 8 : MINE], m[MINE + 16 : MINE + 24]]

    picks = jnp.concatenate(sum([pick(m) for m in [ident] + hot], []), axis=0)
    qmat[...] = product(picks, ymat) * scale

    def from_w(st):
        def produce(zg, i):
            z = zg * 8 + i
            return st.w[z + 1, :, chunk(0)], st.w[z + 1, :, chunk(1)]

        return produce

    for st in both:
        faces_of(from_w(st), st.wfaces, plane_u(st.w))
        sources(st.wfaces, src_w, st is rim)
        inner_sweep(st, st.w, st.base_w, False)
    for st in both:
        all_ghosts(src_w, st)
        each_plane(outer_sweep(st, st.base_w, st.w))

    arrive(share_copies)
    acc = ident * share_w[:, 6:7]
    iwf = iw.astype(F32)
    for f in range(6):
        acc = acc + jnp.where(nb[f : f + 1, 0:WIN] == iwf, share_w[:, (f ^ 1) : (f ^ 1) + 1], 0.0)
    source_row = jnp.sum(acc, axis=0, keepdims=True)
    fixed = jnp.sum(qmat[...] * source_row, axis=1, keepdims=True)
    for n, st in enumerate(both):
        fix = fixed[16 * n : 16 * n + 16]
        st.corr[0] = jnp.broadcast_to(fix, (BLK, LN))
        gains = []
        for f in range(6):
            at = 32 * (f + 1) + 16 * n
            gains.append(jnp.broadcast_to(fixed[at : at + 16] - fix, (BLK, LN)))
        for f in range(4):
            st.corr[1 + f] = gains[f]
        st.corr[5] = jnp.where(even, gains[4], gains[5])

    def third_sweep(st):
        for k in range(12):
            st.ghost[k] += st.corr[1 + GROUP[k]]
        produce = outer_sweep(st, st.base, st.u, st.corr[0])
        faces_of(produce, st.faces, plane_u(st.u))
        sources(st.faces, src_f, st is rim)

    add_remote(X_U2, near_local.at[2], own.ghost)
    third_sweep(own)
    inner_sweep(own, own.u, own.base, True)
    rim_ghosts(2)
    third_sweep(rim)
    inner_sweep(rim, rim.u, rim.base, True)
    for st in both:
        all_ghosts(src_f, st)

    arrive(group_copies)
    part = group_total[0]
    for i in range(1, n_grp):
        part = part + group_total[i]
    level = part[0:1, 0:1] / part[0:1, 64:65]
    level = jnp.broadcast_to(level, (BLK, LN))

    def last_sweep(st):
        add_z(st, st.base)

        def produce(zg, i):
            z = zg * 8 + i
            for h in range(2):
                v = st.base[z, :, chunk(h)] + level * st.w[z + 1, :, chunk(h)]
                v = v + st.gx[z, :, chunk(h)] * spread_x(st.ghost, zg, i, h)
                v = v + st.gy[z, :, chunk(h)] * spread_y(st.ghost, zg, i, h)
                if st is rim:
                    window[2 * z + h, 0:8, :] = v[0:8]
                    window[2 * z + h, 24:32, :] = v[8:16]
                else:
                    window[2 * z + h, 8:24, :] = v

        each_plane(produce)

    for st in both:
        last_sweep(st)

    loads[4].wait()
    owners = own_v[...]
    starts = jnp.sum(jnp.where(owners < me, 1.0, 0.0)).astype(I32)
    count = jnp.sum(jnp.where(owners == me, 1.0, 0.0)).astype(I32)
    at = jnp.clip(starts - BLK * me + 8, 4, 12)
    row24 = lax.broadcasted_iota(I32, (CAP, LN), 0)
    live = row24 < count

    def emit(z):
        for h in range(2):
            lanes = pl.ds(pl.multiple_of(z * 256 + h * LN, LN), LN)
            out[:, lanes] = jnp.where(live, window[2 * z + h, pl.ds(at, CAP), :], 0.0)

    steps(BE, emit)

    for slot in range(N_X):
        finish(face_copies(slot))
    for slot in range(3):
        finish(ghost_copies(slot) + field_copies(slot))
    finish(field_copies(3))
    finish(coupling_copies() + link_copies + share_copies + total_copies + group_copies)


def local(potential, right_side, permeability, new_owner, neighbours):
    n_grp, n_sub = lax.axis_size("grp"), lax.axis_size("sub")
    nblk = new_owner.shape[0]
    vmem = pltpu.VMEM
    plane = (BLK, 256)
    dma = pltpu.SemaphoreType.DMA
    faces = (12, BLK, LN)
    scratch = [
        vmem((2, BLK, 4096), F32),
        vmem((2, BLK, 4096), F32),
        vmem((2, BLK, 4096), F32),
        vmem((nblk // LN, LN), I32),
        vmem((6, nblk), I32),
        vmem((2, BE + 2, *plane), F32),
        vmem((2, BE + 2, *plane), F32),
        vmem((2, BE, *plane), F32),
        vmem((2, BE, *plane), F32),
        vmem((2, BE + 1, *plane), F32),
        vmem((2, BE, *plane), F32),
        vmem((2, BE, *plane), F32),
        vmem((2, BE, *plane), F32),
        vmem((2, 6, BE, *plane), F32),
        vmem((2, BE, *plane), F32),
        vmem((2, BE, *plane), F32),
        vmem((2, BE, *plane), F32),
        vmem((2, 2, *plane), F32),
        vmem((2, BE, *plane), F32),
        vmem((2, BE, *plane), F32),
        vmem((2, *faces), F32),
        vmem((2, *faces), F32),
        vmem((2, *faces), F32),
        vmem((2, *faces), F32),
        vmem((2, 5, BLK, LN), F32),
        vmem((2, 5, BLK, LN), F32),
        vmem((2, 6, BLK, LN), F32),
        vmem(faces, F32),
        vmem(faces, F32),
        vmem(faces, F32),
        vmem((12, 48, LN), F32),
        vmem((12, 48, LN), F32),
        vmem((3, *faces), F32),
        vmem((3, *faces), F32),
        vmem((3, 12, 8, LN), F32),
        vmem((5, BLK, LN), F32),
        vmem((5, 8, LN), F32),
        vmem((LN, 8), F32),
        vmem((224, WIN), F32),
        vmem((WIN, LN), F32),
        vmem((WIN, LN), F32),
        vmem((BLK, LN), F32),
        vmem((N_X, 2, 6, 8, LN), F32),
        vmem((N_X, 2, 6, 8, LN), F32),
        vmem((n_sub, 8, LN), F32),
        vmem((n_grp, 8, LN), F32),
        vmem((32, 40, LN), F32),
        dma((5,)),
        dma((N_X, 2)),
        dma((N_X, 2)),
        dma((4,)),
        dma((4,)),
        dma((4,)),
        dma((4,)),
        dma((n_sub,)),
        dma((n_sub,)),
        dma((n_grp,)),
        dma((n_grp,)),
        dma((4, 2)),
        dma((4, 2)),
        dma((3, 2)),
        dma((3, 2)),
        dma((2,)),
        dma((2,)),
    ]
    return pl.pallas_call(
        functools.partial(kernel, n_grp, n_sub, nblk),
        out_shape=jax.ShapeDtypeStruct((CAP, 4096), F32),
        in_specs=[pl.BlockSpec(memory_space=pl.ANY)] * 5,
        out_specs=pl.BlockSpec(memory_space=pltpu.VMEM),
        scratch_shapes=scratch,
        compiler_params=pltpu.CompilerParams(
            collective_id=0, has_side_effects=True, vmem_limit_bytes=60 * 1024 * 1024
        ),
        cost_estimate=pl.CostEstimate(
            flops=8_000_000, bytes_accessed=1_200_000, transcendentals=0
        ),
        name="cycle",
    )(potential, right_side, permeability, new_owner.reshape(nblk // LN, LN), neighbours)


def solution(mesh):
    in_specs = (P(("grp", "sub"), None), P(("grp", "sub"), None), P(("grp", "sub"), None), P(), P())
    out_specs = P(("grp", "sub"), None)
    return jax.shard_map(local, mesh=mesh, in_specs=in_specs, out_specs=out_specs, check_vma=False)
```

```python
import functools
import types

import jax
import jax.numpy as jnp
from jax import lax
from jax.experimental import pallas as pl
from jax.experimental.pallas import tpu as pltpu
from jax.sharding import PartitionSpec as P

BE = 16
BLK = 16
CAP = 24
LN = 128
RELAX_FINE = 0.8
RELAX_COARSE = 0.7
MESH = pl.DeviceIdType.MESH
F32 = jnp.float32
I32 = jnp.int32
GROUP = (0, 0, 1, 1, 2, 2, 3, 3, 4, 4, 4, 4)
SOURCE = (2, 3, 0, 1, 6, 7, 4, 5)
X_MU, X_U0, X_U1, X_U2 = range(4)
N_X = 4
WIN = 80
MINE = 32


def chunk(h):
    return slice(h * LN, (h + 1) * LN)


def steps(n, body, init=None):
    if init is None:
        lax.fori_loop(0, n, lambda i, _: (body(i), 0)[1], 0, unroll=n)
        return None
    return lax.fori_loop(0, n, body, init, unroll=n)


def kernel(
    n_grp, n_sub, nblk,
    pot, rs, mu, owner, neigh, out,
    mu_s, u0_s, rs_s, own_v, nb_v,
    u_s, w_s, cx_s, cy_s, cz_s, dint_s, t0_s, inv_s, coef_s, rhs_s, gx_s, gy_s, gz_s, base_s, base_w_s,
    faces_s, wfaces_s, ghost_s, cface_s, rel_s, bnd_s, corr_s,
    pface, mu_f, own_mu, src_f, src_w, near_local, near_far, keep,
    rel_local, route, col, qmat, link_w, share_w, rsum,
    send, recv, total, group_total, window, window_w, out_v,
    in_sem, o_sem, x_send, x_recv, l_send, l_recv, s_send, s_recv,
    a_send, a_recv, b_send, b_recv, k_send, k_recv, g_send, g_recv, c_send, c_recv,
):
    def state(k):
        return types.SimpleNamespace(
            mu_v=mu_s.at[k], u0_v=u0_s.at[k], rs_v=rs_s.at[k], u=u_s.at[k], w=w_s.at[k],
            cx=cx_s.at[k], cy=cy_s.at[k], cz=cz_s.at[k], dint=dint_s.at[k], t0=t0_s.at[k],
            inv=inv_s.at[k], coef=coef_s.at[k], rhs=rhs_s.at[k], gx=gx_s.at[k], gy=gy_s.at[k],
            gz=gz_s.at[k], base=base_s.at[k], base_w=base_w_s.at[k], faces=faces_s.at[k],
            wfaces=wfaces_s.at[k], ghost=ghost_s.at[k], cface=cface_s.at[k], rel=rel_s.at[k],
            bnd=bnd_s.at[k], corr=corr_s.at[k],
        )

    own, rim = state(0), state(1)
    both = (own, rim)
    grp, sub = lax.axis_index("grp"), lax.axis_index("sub")
    devices = n_grp * n_sub
    me = grp * n_sub + sub

    def dev(by):
        other = lax.rem(me + by + devices, devices)
        return (lax.div(other, n_sub), lax.rem(other, n_sub))

    def in_group(by):
        return (grp, lax.rem(sub + by + n_sub, n_sub))

    def across(by):
        return (lax.rem(grp + by + n_grp, n_grp), sub)

    def has(by):
        return (me + by >= 0) & (me + by < devices)

    barrier = pltpu.get_barrier_semaphore()

    def greet(to):
        pl.semaphore_signal(barrier, inc=1, device_id=to, device_id_type=MESH)

    greeted = n_sub - 1 + n_grp - 1
    for by in (1, -1, 2, -2):
        pl.when(has(by))(functools.partial(greet, dev(by)))
        greeted = greeted + has(by).astype(I32)
    for by in range(1, n_sub):
        greet(in_group(by))
    for by in range(1, n_grp):
        greet(across(by))

    loads = [
        pltpu.make_async_copy(a, b, in_sem.at[i])
        for i, (a, b) in enumerate(
            ((mu, own.mu_v), (neigh, nb_v), (pot, own.u0_v), (rs, own.rs_v), (owner, own_v))
        )
    ]
    for copy in loads:
        copy.start()

    lane = lax.broadcasted_iota(I32, (BLK, LN), 1)
    xpos = lane & 15
    yrow = lane >> 4
    row = lax.broadcasted_iota(I32, (BLK, LN), 0)
    lane8 = lax.broadcasted_iota(I32, (8, LN), 1)
    row8 = lax.broadcasted_iota(I32, (8, LN), 0)
    x_first, x_last = xpos == 0, xpos == BE - 1
    x_face = x_first | x_last
    y_first, y_last = lane < BE, lane >= LN - BE
    even = (lane & 1) == 0
    zero = jnp.zeros((BLK, LN), F32)

    def turn(v, by):
        if isinstance(by, int):
            by = by % LN
            return v if by == 0 else pltpu.roll(v, by, 1)
        return pltpu.roll(v, by & (LN - 1), 1)

    def lower_y(v0, v1):
        a, b = turn(v0, BE), turn(v1, BE)
        return a, jnp.where(y_first, a, b)

    def upper_y(v0, v1):
        a, b = turn(v0, -BE), turn(v1, -BE)
        return jnp.where(y_last, b, a), b

    def remote(src, dst, a, b, to):
        return pltpu.make_async_remote_copy(
            src_ref=src, dst_ref=dst, send_sem=a, recv_sem=b, device_id=to, device_id_type=MESH
        )

    def faces_of(produce, faces_ref, plane):
        for zg in range(2):
            def body(i, carry, zg=zg):
                x0, x1, y2, y3 = carry
                v0, v1 = produce(zg, i)
                here = (xpos == 2 * i) | (xpos == ((2 * i + 15) & 15))
                x0 = jnp.where(here, turn(v0, 2 * i), x0)
                x1 = jnp.where(here, turn(v1, 2 * i), x1)
                line = yrow == i
                y2 = jnp.where(line, turn(v0, BE * i), y2)
                y3 = jnp.where(line, turn(v1, BE * i + BE), y3)
                return x0, x1, y2, y3

            x0, x1, y2, y3 = steps(8, body, (zero, zero, zero, zero))
            faces_ref[8 + 2 * zg] = x0
            faces_ref[9 + 2 * zg] = x1
            faces_ref[4 + zg] = y2
            faces_ref[6 + zg] = y3
        for h in range(2):
            faces_ref[h] = plane(0, h)
            faces_ref[2 + h] = plane(BE - 1, h)

    def sources(faces_ref, src_ref, is_rim=False):
        for k in range(12):
            if k < 8:
                v = faces_ref[SOURCE[k]]
            else:
                x = faces_ref[k]
                v = jnp.where(even, turn(x, -15), turn(x, 15))
            if is_rim:
                src_ref[k, 8:16, :] = v[0:8]
                src_ref[k, 32:40, :] = v[8:16]
            else:
                src_ref[k, 16:32, :] = v

    def send_faces(src_ref, slot):
        for m in range(6):
            pair = []
            for k in (2 * m, 2 * m + 1):
                edge = jnp.where(row8 < 4, src_ref[k, 16:24, :], src_ref[k, 24:32, :])
                way = route[GROUP[k]]
                d = jnp.zeros((8, LN), F32)
                for r in (4,) if k < 4 else range(1, 8):
                    d = jnp.where(way == r, pltpu.roll(edge, r, 0), d)
                pair.append(d)
                if slot:
                    keep[slot - 1, k] = d
            d0, d1 = pair
            send[slot, 0, m] = jnp.where(row8 < 4, d0, pltpu.roll(d1, 4, 0))
            send[slot, 1, m] = jnp.where(row8 < 4, pltpu.roll(d0, 4, 0), d1)
        start(face_copies(slot))

    def face_copies(slot):
        return [
            (
                remote(
                    send.at[slot, way],
                    recv.at[slot, way],
                    x_send.at[slot, way],
                    x_recv.at[slot, way],
                    dev(1 - 2 * way),
                ),
                1 - 2 * way,
            )
            for way in range(2)
        ]

    def local_ghosts(src_ref, ghost_ref):
        for k in range(12):
            r = rel_local[GROUP[k]]
            g = zero
            for by in (-4, 4) if k < 4 else range(-4, 5):
                g = jnp.where(r == by, src_ref[k, 16 + by : 32 + by, :], g)
            ghost_ref[k] = g

    def all_ghosts(src_ref, st):
        for k in range(12):
            r = st.rel[GROUP[k]]
            tops = (8, 32) if st is rim else (16, 24)
            for t in range(2):
                g = jnp.zeros((8, LN), F32)
                rt = r[8 * t : 8 * t + 8]
                for by in (-4, 4) if k < 4 else range(-4, 5):
                    g = jnp.where(rt == by, src_ref[k, tops[t] + by : tops[t] + by + 8, :], g)
                st.ghost[k, 8 * t : 8 * t + 8, :] = g

    def add_remote(slot, near_ref, ghost_ref):
        arrive(face_copies(slot))
        for m in range(6):
            lo, hi = recv[slot, 0, m], recv[slot, 1, m]
            lo1, hi0 = pltpu.roll(lo, 4, 0), pltpu.roll(hi, 4, 0)
            a, b = 2 * m, 2 * m + 1
            ghost_ref[a, 0:8, :] = near_ref[a, 0:8, :] + jnp.where(row8 < 4, lo, 0.0)
            ghost_ref[b, 0:8, :] = near_ref[b, 0:8, :] + jnp.where(row8 < 4, lo1, 0.0)
            ghost_ref[a, 8:16, :] = near_ref[a, 8:16, :] + jnp.where(row8 < 4, 0.0, hi0)
            ghost_ref[b, 8:16, :] = near_ref[b, 8:16, :] + jnp.where(row8 < 4, 0.0, hi)

    def rows_both_ways(src, dst, a, b):
        return [
            (remote(src(8), dst(0), a.at[0], b.at[0], dev(1)), 1),
            (remote(src(0), dst(8), a.at[1], b.at[1], dev(-1)), -1),
        ]

    def field_copies(k):
        ref = (mu_s, u0_s, rs_s, u0_s)[k]
        lanes = {1: pl.ds(0, 2048), 3: pl.ds(2048, 2048)}.get(k, pl.ds(0, 4096))
        return rows_both_ways(
            lambda r: ref.at[0, pl.ds(r, 8), lanes],
            lambda r: ref.at[1, pl.ds(r, 8), lanes],
            k_send.at[k],
            k_recv.at[k],
        )

    def ghost_copies(slot):
        return rows_both_ways(
            lambda r: near_local.at[slot, :, pl.ds(r, 8)],
            lambda r: near_far.at[slot, :, pl.ds(r, 8)],
            g_send.at[slot],
            g_recv.at[slot],
        )

    def coupling_copies():
        return rows_both_ways(
            lambda r: cface_s.at[0, :, pl.ds(r, 8)],
            lambda r: cface_s.at[1, :, pl.ds(r, 8)],
            c_send,
            c_recv,
        )

    def start(copies):
        for copy, by in copies:
            if by is None:
                copy.start()
            else:
                pl.when(has(by))(copy.start)

    def arrive(copies):
        for copy, by in copies:
            if by is None:
                copy.wait_recv()
            else:
                pl.when(has(-by))(copy.wait_recv)

    def finish(copies):
        for copy, by in copies:
            if by is None:
                copy.wait_send()
            else:
                pl.when(has(by))(copy.wait_send)

    def rim_ghosts(slot):
        arrive(ghost_copies(slot))
        for k in range(12):
            d = keep[slot, k]
            rim.ghost[k, 0:8, :] = near_far[slot, k, 0:8, :] + jnp.where(row8 < 4, 0.0, d)
            rim.ghost[k, 8:16, :] = near_far[slot, k, 8:16, :] + jnp.where(row8 < 4, d, 0.0)

    def spread_x(faces_ref, zg, i, h):
        return turn(faces_ref[8 + 2 * zg + h], LN - 2 * i)

    def spread_y(faces_ref, zg, i, h):
        return turn(faces_ref[(4, 6)[h] + zg], LN - BE * i - (0, BE)[h])

    first = BLK * me - MINE
    loads[1].wait()
    low = lax.div(first + LN, LN) - 1
    shift = first - low * LN
    tiles = nblk // LN

    def table(k):
        at = pl.multiple_of(lax.rem(k + tiles, tiles) * LN, LN)
        rows6 = nb_v[:, pl.ds(at, LN)]
        return jnp.concatenate([rows6, jnp.full((2, LN), -1, I32)], axis=0)

    back = LN - shift
    ta, tb = turn(table(low), back), turn(table(low + 1), back)
    ids = first + lane8
    nb = jnp.where(lane8 < back, ta, tb)
    nb = jnp.where((nb >= 0) & (ids >= 0) & (ids < nblk), nb - first, -1000).astype(F32)
    nbt = nb.T
    col[...] = nbt

    def columns(f, lo, n):
        return jnp.broadcast_to(col[lo : lo + n, f : f + 1], (n, LN))

    rowf = row.astype(F32)
    row8f = row8.astype(F32)
    rim_row = jnp.where(row < 8, rowf + (MINE - 8.0), rowf + (MINE + 8.0))
    far = jnp.zeros((BLK, LN), F32) + 99.0
    rels, routes, edges, full, rim_full, rim_edges = [], [], [], [], [], []
    for f in range(6):
        to = columns(f, MINE, 16)
        step = to - float(MINE) - rowf
        near = (to >= float(MINE)) & (to < MINE + 16.0)
        rels.append(jnp.where(near, step, far))
        full.append(step)
        edges.append(jnp.where(to < 0.0, 1.0, 0.0))
        before, after = columns(f, MINE - 8, 8), columns(f, MINE + 16, 8)
        to = jnp.concatenate([before, after], axis=0)
        rim_full.append(to - rim_row)
        rim_edges.append(jnp.where(to < 0.0, 1.0, 0.0))
        to8 = jnp.where(row8 < 4, after, before)
        j = jnp.where(row8 < 4, to8 - (MINE + 8.0), to8 - float(MINE))
        ok = jnp.where(row8 < 4, jnp.where(j >= 4.0, 1.0, 0.0), jnp.where(j >= 0.0, 1.0, 0.0))
        ok = ok * jnp.where(row8 < 4, jnp.where(j < 8.0, 1.0, 0.0), jnp.where(j < 4.0, 1.0, 0.0))
        r = row8f - j
        routes.append(jnp.where(ok > 0.5, jnp.where(r < 0.0, r + 8.0, r), 99.0))
    even8 = (lane8 & 1) == 0
    for g in range(4):
        rel_local[g], route[g] = rels[g], routes[g]
        own.rel[g], own.bnd[g] = full[g], edges[g]
        rim.rel[g], rim.bnd[g] = rim_full[g], rim_edges[g]
    rel_local[4] = jnp.where(even, rels[4], rels[5])
    route[4] = jnp.where(even8, routes[4], routes[5])
    own.rel[4] = jnp.where(even, full[4], full[5])
    own.bnd[4] = jnp.where(even, edges[4], edges[5])
    rim.rel[4] = jnp.where(even, rim_full[4], rim_full[5])
    rim.bnd[4] = jnp.where(even, rim_edges[4], rim_edges[5])
    for st, e in ((own, edges), (rim, rim_edges)):
        st.bx = jnp.where(x_first, e[4], jnp.where(x_last, e[5], 0.0))
        st.by = (jnp.where(y_first, e[2], 0.0), jnp.where(y_last, e[3], 0.0))

    def fill_way(way):
        for slot in range(N_X):
            for m in range(6):
                recv[slot, way, m] = jnp.zeros((8, LN), F32)

    def fill_blocks(by):
        at = MINE + 16 * by
        link_w[at : at + 16] = jnp.ones((16, LN), F32)
        share_w[at : at + 16] = jnp.zeros((16, LN), F32)

    for way in range(2):
        pl.when(jnp.logical_not(has(2 * way - 1)))(functools.partial(fill_way, way))
    for by in (1, -1, 2, -2):
        pl.when(jnp.logical_not(has(by)))(functools.partial(fill_blocks, by))

    def plane_of(ref):
        return lambda z, h: ref[:, z * 256 + h * LN : z * 256 + (h + 1) * LN]

    def from_input(ref, store=None):
        def produce(zg, i):
            at = pl.multiple_of((zg * 8 + i) * 256, 256)
            v0, v1 = ref[:, pl.ds(at, LN)], ref[:, pl.ds(at + LN, LN)]
            if store is not None:
                store[zg * 8 + i + 1, :, chunk(0)] = v0
                store[zg * 8 + i + 1, :, chunk(1)] = v1
            return v0, v1

        return produce

    loads[0].wait()
    faces_of(from_input(own.mu_v), own_mu, plane_of(own.mu_v))
    sources(own_mu, src_w)
    pl.semaphore_wait(barrier, greeted)
    send_faces(src_w, X_MU)
    loads[2].wait()
    faces_of(from_input(own.u0_v, own.u), own.faces, plane_of(own.u0_v))
    sources(own.faces, src_f)
    send_faces(src_f, X_U0)
    local_ghosts(src_f, near_local.at[0])
    loads[3].wait()
    start(field_copies(0))
    start(field_copies(2))
    start(field_copies(3))

    local_ghosts(src_w, mu_f)
    for st in both:
        for ref in (st.u, st.w):
            ref[0] = jnp.zeros((BLK, 256), F32)
            ref[BE + 1] = jnp.zeros((BLK, 256), F32)
        st.cz[0] = jnp.zeros((BLK, 256), F32)
        st.cz[BE] = jnp.zeros((BLK, 256), F32)

    def mean(a, b):
        return 2.0 * a * b / (a + b)

    def inner_couplings(st):
        def body(z):
            at = pl.multiple_of(z * 256, 256)
            m0, m1 = st.mu_v[:, pl.ds(at, LN)], st.mu_v[:, pl.ds(at + LN, LN)]
            y0, y1 = lower_y(m0, m1)
            st.cx[z, :, chunk(0)] = jnp.where(x_first, 0.0, mean(m0, turn(m0, 1)))
            st.cx[z, :, chunk(1)] = jnp.where(x_first, 0.0, mean(m1, turn(m1, 1)))
            st.cy[z, :, chunk(0)] = jnp.where(y_first, 0.0, mean(m0, y0))
            st.cy[z, :, chunk(1)] = mean(m1, y1)

        def across_z(z):
            at = pl.multiple_of(z * 256, 256)
            st.cz[z + 1] = mean(st.mu_v[:, pl.ds(at, 256)], st.mu_v[:, pl.ds(at + 256, 256)])

        steps(BE, body)
        steps(BE - 1, across_z)

    inner_couplings(own)

    def around(st, z):
        cx0, cx1 = st.cx[z, :, chunk(0)], st.cx[z, :, chunk(1)]
        cy0, cy1 = st.cy[z, :, chunk(0)], st.cy[z, :, chunk(1)]
        uy0, uy1 = upper_y(cy0, cy1)
        uy1 = jnp.where(y_last, 0.0, uy1)
        lo = (st.cz[z, :, chunk(0)], st.cz[z, :, chunk(1)])
        up = (st.cz[z + 1, :, chunk(0)], st.cz[z + 1, :, chunk(1)])
        return (
            (lo[0], up[0], cy0, uy0, cx0, turn(cx0, -1)),
            (lo[1], up[1], cy1, uy1, cx1, turn(cx1, -1)),
        )

    def beside(ref, z):
        v0, v1 = ref[z + 1, :, chunk(0)], ref[z + 1, :, chunk(1)]
        l0, l1 = lower_y(v0, v1)
        p0, p1 = upper_y(v0, v1)
        return (v0, v1), (
            (ref[z, :, chunk(0)], ref[z + 2, :, chunk(0)], l0, p0, turn(v0, 1), turn(v0, -1)),
            (ref[z, :, chunk(1)], ref[z + 2, :, chunk(1)], l1, p1, turn(v1, 1), turn(v1, -1)),
        )

    def first_terms(st):
        def body(z, acc):
            c = around(st, z)
            _, n = beside(st.u, z)
            for h in range(2):
                at = pl.multiple_of(z * 256 + h * LN, LN)
                r = st.rs_v[:, pl.ds(at, LN)]
                d = c[h][0]
                t = r + c[h][0] * n[h][0]
                for f in range(1, 6):
                    d = d + c[h][f]
                    t = t + c[h][f] * n[h][f]
                st.dint[z, :, chunk(h)] = d
                st.t0[z, :, chunk(h)] = t
                acc = acc + r
            return acc

        return steps(BE, body, zero)

    acc = first_terms(own)
    rsum[...] = jnp.broadcast_to(jnp.sum(acc, axis=1, keepdims=True), (BLK, LN))

    add_remote(X_MU, mu_f, own.ghost)
    for k in range(12):
        m = own_mu[k]
        g = jnp.where(own.bnd[GROUP[k]] > 0.5, m, own.ghost[k])
        own.cface[k] = mean(m, g)
    add_remote(X_U0, near_local.at[0], own.ghost)

    def add_first_z(st):
        for k in range(12):
            pface[k] = st.cface[k] * st.ghost[k]
        for h in range(2):
            st.dint[0, :, chunk(h)] += st.cface[h]
            st.dint[BE - 1, :, chunk(h)] += st.cface[2 + h]
            st.t0[0, :, chunk(h)] += pface[h]
            st.t0[BE - 1, :, chunk(h)] += pface[2 + h]

    y_face = (y_first, y_last)

    def sweep_first(st):
        def produce(zg, i):
            z = zg * 8 + i
            vs = []
            for h in range(2):
                d = st.dint[z, :, chunk(h)]
                t = st.t0[z, :, chunk(h)]
                d = d + jnp.where(x_face, spread_x(st.cface, zg, i, h), 0.0)
                d = d + jnp.where(y_face[h], spread_y(st.cface, zg, i, h), 0.0)
                t = t + jnp.where(x_face, spread_x(pface, zg, i, h), 0.0)
                t = t + jnp.where(y_face[h], spread_y(pface, zg, i, h), 0.0)
                q = RELAX_FINE / d
                st.inv[z, :, chunk(h)] = q
                v = (1.0 - RELAX_FINE) * st.u[z + 1, :, chunk(h)] + q * t
                st.u[z + 1, :, chunk(h)] = v
                vs.append(v)
            return vs

        return produce

    def each_plane(produce):
        for zg in range(2):
            steps(8, lambda i, zg=zg: (produce(zg, i), None)[1])

    def plane_u(ref):
        return lambda z, h: ref[z + 1, :, chunk(h)]

    add_first_z(own)
    faces_of(sweep_first(own), own.faces, plane_u(own.u))
    sources(own.faces, src_f)
    send_faces(src_f, X_U1)
    start(field_copies(1))
    start(ghost_copies(0))

    def coefficients(st):
        for h in range(2):
            st.gz[0, :, chunk(h)] = st.cface[h] * st.inv[0, :, chunk(h)]
            st.gz[1, :, chunk(h)] = st.cface[2 + h] * st.inv[BE - 1, :, chunk(h)]

        def produce(zg, i):
            z = zg * 8 + i
            c = around(st, z)
            for h in range(2):
                q = st.inv[z, :, chunk(h)]
                for f in range(6):
                    st.coef[f, z, :, chunk(h)] = c[h][f] * q
                at = pl.multiple_of(z * 256 + h * LN, LN)
                st.rhs[z, :, chunk(h)] = st.rs_v[:, pl.ds(at, LN)] * q
                fx = jnp.where(x_face, spread_x(st.cface, zg, i, h), 0.0) * q
                fy = jnp.where(y_face[h], spread_y(st.cface, zg, i, h), 0.0) * q
                st.gx[z, :, chunk(h)] = fx
                st.gy[z, :, chunk(h)] = fy
                st.w[z + 1, :, chunk(h)] = 1.0 - fx * st.bx - fy * st.by[h]

        each_plane(produce)
        for h in range(2):
            st.w[1, :, chunk(h)] -= st.gz[0, :, chunk(h)] * st.bnd[0]
            st.w[BE, :, chunk(h)] -= st.gz[1, :, chunk(h)] * st.bnd[1]

    def inner_sweep(st, ref, base_ref, with_rhs):
        def body(z):
            v, n = beside(ref, z)
            for h in range(2):
                b = (1.0 - RELAX_FINE) * v[h]
                if with_rhs:
                    b = b + st.rhs[z, :, chunk(h)]
                for f in range(6):
                    b = b + st.coef[f, z, :, chunk(h)] * n[h][f]
                base_ref[z, :, chunk(h)] = b

        steps(BE, body)

    def add_z(st, base_ref):
        for h in range(2):
            base_ref[0, :, chunk(h)] += st.gz[0, :, chunk(h)] * st.ghost[h]
            base_ref[BE - 1, :, chunk(h)] += st.gz[1, :, chunk(h)] * st.ghost[2 + h]

    def outer_sweep(st, base_ref, ref, fix=None):
        add_z(st, base_ref)

        def produce(zg, i):
            z = zg * 8 + i
            vs = []
            for h in range(2):
                v = base_ref[z, :, chunk(h)]
                if fix is not None:
                    v = v + fix
                v = v + st.gx[z, :, chunk(h)] * spread_x(st.ghost, zg, i, h)
                v = v + st.gy[z, :, chunk(h)] * spread_y(st.ghost, zg, i, h)
                ref[z + 1, :, chunk(h)] = v
                vs.append(v)
            return vs

        return produce

    local_ghosts(src_f, near_local.at[1])
    coefficients(own)
    inner_sweep(own, own.u, own.base, True)
    start(ghost_copies(1))
    start(coupling_copies())

    def face_sums(value):
        sums = []
        for f in range(4):
            s = value(2 * f) + value(2 * f + 1)
            sums.append(jnp.sum(s, axis=1, keepdims=True))
        s = value(8) + value(9) + value(10) + value(11)
        sums.append(jnp.sum(jnp.where(even, s, 0.0), axis=1, keepdims=True))
        sums.append(jnp.sum(jnp.where(even, 0.0, s), axis=1, keepdims=True))
        return sums

    links = face_sums(lambda k: own.cface[k])
    tile = zero
    link_total = links[0]
    for f in range(6):
        tile = jnp.where(lane == f, links[f], tile)
        if f:
            link_total = link_total + links[f]
    link_w[MINE : MINE + 16] = tile

    def spread_blocks(ref, a, b):
        mine = ref.at[pl.ds(MINE, 16)]
        return [
            (remote(mine, ref.at[pl.ds(MINE - 16 * by, 16)], a.at[i], b.at[i], dev(by)), by)
            for i, by in enumerate((1, -1, 2, -2))
        ]

    link_copies = spread_blocks(link_w, l_send, l_recv)
    start(link_copies)


    add_remote(X_U1, near_local.at[1], own.ghost)
    faces_of(outer_sweep(own, own.base, own.u), own.faces, plane_u(own.u))
    sums = face_sums(lambda k: own.cface[k] * own.faces[k])
    left = rsum[:, 0:1]
    group_left = left
    tile = zero
    for f in range(6):
        tile = jnp.where(lane == f, sums[f], tile)
        left = left - sums[f]
        group_left = group_left - sums[f] * edges[f][:, 0:1]
    share_w[MINE : MINE + 16] = jnp.where(lane == 6, left, tile)
    total[0] = jnp.where(
        lane8 < 64,
        jnp.sum(group_left, axis=0, keepdims=True),
        jnp.sum(link_total, axis=0, keepdims=True),
    )
    total_copies = [
        (remote(total.at[0], total.at[i], a_send.at[i], a_recv.at[i], in_group(i)), None)
        for i in range(1, n_sub)
    ]
    start(total_copies)

    sources(own.faces, src_f)
    send_faces(src_f, X_U2)
    share_copies = spread_blocks(share_w, s_send, s_recv)
    start(share_copies)
    local_ghosts(src_f, near_local.at[2])
    start(ghost_copies(2))

    inner_sweep(own, own.u, own.base, True)
    arrive(field_copies(0))
    inner_couplings(rim)
    arrive(field_copies(1) + field_copies(2) + field_copies(3))
    each_plane(from_input(rim.u0_v, rim.u))
    first_terms(rim)
    arrive(coupling_copies())
    rim_ghosts(0)
    add_first_z(rim)
    each_plane(sweep_first(rim))
    coefficients(rim)
    inner_sweep(rim, rim.u, rim.base, True)
    rim_ghosts(1)
    each_plane(outer_sweep(rim, rim.base, rim.u))
    inner_sweep(rim, rim.u, rim.base, True)

    arrive(total_copies)
    part = total[0]
    for i in range(1, n_sub):
        part = part + total[i]
    group_total[0] = part
    group_copies = [
        (remote(group_total.at[0], group_total.at[i], b_send.at[i], b_recv.at[i], across(i)), None)
        for i in range(1, n_grp)
    ]
    start(group_copies)

    arrive(link_copies)
    iw = lax.broadcasted_iota(I32, (WIN, WIN), 0)
    lw = lax.broadcasted_iota(I32, (WIN, WIN), 1)
    lwf = lw.astype(F32)
    diagonal = link_w[:, 0:1]
    for f in range(1, 6):
        diagonal = diagonal + link_w[:, f : f + 1]
    gain = RELAX_COARSE / diagonal
    ident = jnp.where(iw == lw, 1.0, 0.0)
    hot = [jnp.where(col[0:WIN, f : f + 1] == lwf, 1.0, 0.0) for f in range(6)]
    gmat = link_w[:, 0:1] * hot[0]
    for f in range(1, 6):
        gmat = gmat + link_w[:, f : f + 1] * hot[f]
    gmat = gmat * gain + (1.0 - RELAX_COARSE) * ident

    def product(a, b):
        return lax.dot_general(
            a,
            b,
            (((1,), (0,)), ((), ())),
            precision=lax.Precision.HIGHEST,
            preferred_element_type=F32,
        )

    ymat = ident + gmat
    ymat = ident + product(ymat, gmat)
    ymat = ident + product(ymat, gmat)
    scale = jnp.sum(ident * gain, axis=0, keepdims=True)

    def pick(m):
        return [m[MINE : MINE + 16], m[MINE - 8 : MINE], m[MINE + 16 : MINE + 24]]

    picks = jnp.concatenate(sum([pick(m) for m in [ident] + hot], []), axis=0)
    qmat[...] = product(picks, ymat) * scale

    def window_sweep(st, base_ref, win):
        add_z(st, base_ref)

        def produce(zg, i):
            z = zg * 8 + i
            for h in range(2):
                v = base_ref[z, :, chunk(h)]
                v = v + st.gx[z, :, chunk(h)] * spread_x(st.ghost, zg, i, h)
                v = v + st.gy[z, :, chunk(h)] * spread_y(st.ghost, zg, i, h)
                if st is rim:
                    win[2 * z + h, 0:8, :] = v[0:8]
                    win[2 * z + h, 24:32, :] = v[8:16]
                else:
                    win[2 * z + h, 8:24, :] = v

        each_plane(produce)

    def from_w(st):
        def produce(zg, i):
            z = zg * 8 + i
            return st.w[z + 1, :, chunk(0)], st.w[z + 1, :, chunk(1)]

        return produce

    for st in both:
        faces_of(from_w(st), st.wfaces, plane_u(st.w))
        sources(st.wfaces, src_w, st is rim)
        inner_sweep(st, st.w, st.base_w, False)
    for st in both:
        all_ghosts(src_w, st)
        window_sweep(st, st.base_w, window_w)

    arrive(share_copies)
    acc = ident * share_w[:, 6:7]
    iwf = iw.astype(F32)
    for f in range(6):
        acc = acc + jnp.where(nb[f : f + 1, 0:WIN] == iwf, share_w[:, (f ^ 1) : (f ^ 1) + 1], 0.0)
    source_row = jnp.sum(acc, axis=0, keepdims=True)
    fixed = jnp.sum(qmat[...] * source_row, axis=1, keepdims=True)
    for n, st in enumerate(both):
        fix = fixed[16 * n : 16 * n + 16]
        st.corr[0] = jnp.broadcast_to(fix, (BLK, LN))
        gains = []
        for f in range(6):
            at = 32 * (f + 1) + 16 * n
            gains.append(jnp.broadcast_to(fixed[at : at + 16] - fix, (BLK, LN)))
        for f in range(4):
            st.corr[1 + f] = gains[f]
        st.corr[5] = jnp.where(even, gains[4], gains[5])

    def third_sweep(st):
        for k in range(12):
            st.ghost[k] += st.corr[1 + GROUP[k]]
        produce = outer_sweep(st, st.base, st.u, st.corr[0])
        faces_of(produce, st.faces, plane_u(st.u))
        sources(st.faces, src_f, st is rim)

    add_remote(X_U2, near_local.at[2], own.ghost)
    third_sweep(own)
    inner_sweep(own, own.u, own.base, True)
    rim_ghosts(2)
    third_sweep(rim)
    inner_sweep(rim, rim.u, rim.base, True)
    for st in both:
        all_ghosts(src_f, st)

    for st in both:
        window_sweep(st, st.base, window)

    loads[4].wait()
    owners = own_v[...]
    starts = jnp.sum(jnp.where(owners < me, 1.0, 0.0)).astype(I32)
    count = jnp.sum(jnp.where(owners == me, 1.0, 0.0)).astype(I32)
    at = jnp.clip(starts - BLK * me + 8, 4, 12)
    row24 = lax.broadcasted_iota(I32, (CAP, LN), 0)
    live = row24 < count

    arrive(group_copies)
    part = group_total[0]
    for i in range(1, n_grp):
        part = part + group_total[i]
    level = part[0:1, 0:1] / part[0:1, 64:65]
    level = jnp.broadcast_to(level, (CAP, LN))

    out_copies = []
    for q in range(4):
        def emit(i, q=q):
            z = 4 * q + i
            for h in range(2):
                lanes = pl.ds(pl.multiple_of(z * 256 + h * LN, LN), LN)
                rows = pl.ds(at, CAP)
                v = window[2 * z + h, rows, :] + level * window_w[2 * z + h, rows, :]
                out_v[:, lanes] = jnp.where(live, v, 0.0)

        steps(4, emit)
        part = pl.ds(1024 * q, 1024)
        copy = pltpu.make_async_copy(out_v.at[:, part], out.at[:, part], o_sem.at[q])
        copy.start()
        out_copies.append(copy)

    for slot in range(N_X):
        finish(face_copies(slot))
    for slot in range(3):
        finish(ghost_copies(slot) + field_copies(slot))
    finish(field_copies(3))
    finish(coupling_copies() + link_copies + share_copies + total_copies + group_copies)
    for copy in out_copies:
        copy.wait()


def local(potential, right_side, permeability, new_owner, neighbours):
    n_grp, n_sub = lax.axis_size("grp"), lax.axis_size("sub")
    nblk = new_owner.shape[0]
    vmem = pltpu.VMEM
    plane = (BLK, 256)
    dma = pltpu.SemaphoreType.DMA
    faces = (12, BLK, LN)
    scratch = [
        vmem((2, BLK, 4096), F32),
        vmem((2, BLK, 4096), F32),
        vmem((2, BLK, 4096), F32),
        vmem((nblk // LN, LN), I32),
        vmem((6, nblk), I32),
        vmem((2, BE + 2, *plane), F32),
        vmem((2, BE + 2, *plane), F32),
        vmem((2, BE, *plane), F32),
        vmem((2, BE, *plane), F32),
        vmem((2, BE + 1, *plane), F32),
        vmem((2, BE, *plane), F32),
        vmem((2, BE, *plane), F32),
        vmem((2, BE, *plane), F32),
        vmem((2, 6, BE, *plane), F32),
        vmem((2, BE, *plane), F32),
        vmem((2, BE, *plane), F32),
        vmem((2, BE, *plane), F32),
        vmem((2, 2, *plane), F32),
        vmem((2, BE, *plane), F32),
        vmem((2, BE, *plane), F32),
        vmem((2, *faces), F32),
        vmem((2, *faces), F32),
        vmem((2, *faces), F32),
        vmem((2, *faces), F32),
        vmem((2, 5, BLK, LN), F32),
        vmem((2, 5, BLK, LN), F32),
        vmem((2, 6, BLK, LN), F32),
        vmem(faces, F32),
        vmem(faces, F32),
        vmem(faces, F32),
        vmem((12, 48, LN), F32),
        vmem((12, 48, LN), F32),
        vmem((3, *faces), F32),
        vmem((3, *faces), F32),
        vmem((3, 12, 8, LN), F32),
        vmem((5, BLK, LN), F32),
        vmem((5, 8, LN), F32),
        vmem((LN, 8), F32),
        vmem((224, WIN), F32),
        vmem((WIN, LN), F32),
        vmem((WIN, LN), F32),
        vmem((BLK, LN), F32),
        vmem((N_X, 2, 6, 8, LN), F32),
        vmem((N_X, 2, 6, 8, LN), F32),
        vmem((n_sub, 8, LN), F32),
        vmem((n_grp, 8, LN), F32),
        vmem((32, 40, LN), F32),
        vmem((32, 40, LN), F32),
        vmem((CAP, 4096), F32),
        dma((5,)),
        dma((4,)),
        dma((N_X, 2)),
        dma((N_X, 2)),
        dma((4,)),
        dma((4,)),
        dma((4,)),
        dma((4,)),
        dma((n_sub,)),
        dma((n_sub,)),
        dma((n_grp,)),
        dma((n_grp,)),
        dma((4, 2)),
        dma((4, 2)),
        dma((3, 2)),
        dma((3, 2)),
        dma((2,)),
        dma((2,)),
    ]
    return pl.pallas_call(
        functools.partial(kernel, n_grp, n_sub, nblk),
        out_shape=jax.ShapeDtypeStruct((CAP, 4096), F32),
        in_specs=[pl.BlockSpec(memory_space=pl.ANY)] * 5,
        out_specs=pl.BlockSpec(memory_space=pl.ANY),
        scratch_shapes=scratch,
        compiler_params=pltpu.CompilerParams(
            collective_id=0, has_side_effects=True, vmem_limit_bytes=60 * 1024 * 1024
        ),
        cost_estimate=pl.CostEstimate(
            flops=8_000_000, bytes_accessed=1_200_000, transcendentals=0
        ),
        name="cycle",
    )(potential, right_side, permeability, new_owner.reshape(nblk // LN, LN), neighbours)


def solution(mesh):
    in_specs = (P(("grp", "sub"), None), P(("grp", "sub"), None), P(("grp", "sub"), None), P(), P())
    out_specs = P(("grp", "sub"), None)
    return jax.shard_map(local, mesh=mesh, in_specs=in_specs, out_specs=out_specs, check_vma=False)
```

```python
import functools
import types

import jax
import jax.numpy as jnp
from jax import lax
from jax.experimental import pallas as pl
from jax.experimental.pallas import tpu as pltpu
from jax.sharding import PartitionSpec as P

BE = 16
BLK = 16
CAP = 24
LN = 128
RELAX_FINE = 0.8
RELAX_COARSE = 0.7
MESH = pl.DeviceIdType.MESH
F32 = jnp.float32
I32 = jnp.int32
GROUP = (0, 0, 1, 1, 2, 2, 3, 3, 4, 4, 4, 4)
SOURCE = (2, 3, 0, 1, 6, 7, 4, 5)
X_MU, X_U0, X_U1, X_U2 = range(4)
N_X = 4
WIN = 80
MINE = 32


def chunk(h):
    return slice(h * LN, (h + 1) * LN)


def steps(n, body, init=None):
    if init is None:
        lax.fori_loop(0, n, lambda i, _: (body(i), 0)[1], 0, unroll=n)
        return None
    return lax.fori_loop(0, n, body, init, unroll=n)


def kernel(
    n_grp, n_sub, nblk,
    pot, rs, mu, owner, neigh, out,
    mu_s, u0_s, rs_s, own_v, nb_v,
    u_s, w_s, cx_s, cy_s, cz_s, dint_s, t0_s, inv_s, coef_s, rhs_s, gx_s, gy_s, gz_s, base_s, base_w_s,
    faces_s, wfaces_s, ghost_s, cface_s, rel_s, bnd_s, corr_s,
    pface, mu_f, own_mu, src_f, src_w, near_local, near_far, keep,
    rel_local, route, col, qmat, link_w, share_w, rsum,
    send, recv, total, group_total, window, window_w, out_v,
    in_sem, o_sem, x_send, x_recv, l_send, l_recv, s_send, s_recv,
    a_send, a_recv, b_send, b_recv, k_send, k_recv, g_send, g_recv, c_send, c_recv,
):
    def state(k):
        return types.SimpleNamespace(
            mu_v=mu_s.at[k], u0_v=u0_s.at[k], rs_v=rs_s.at[k], u=u_s.at[k], w=w_s.at[k],
            cx=cx_s.at[k], cy=cy_s.at[k], cz=cz_s.at[k], dint=dint_s.at[k], t0=t0_s.at[k],
            inv=inv_s.at[k], coef=coef_s.at[k], rhs=rhs_s.at[k], gx=gx_s.at[k], gy=gy_s.at[k],
            gz=gz_s.at[k], base=base_s.at[k], base_w=base_w_s.at[k], faces=faces_s.at[k],
            wfaces=wfaces_s.at[k], ghost=ghost_s.at[k], cface=cface_s.at[k], rel=rel_s.at[k],
            bnd=bnd_s.at[k], corr=corr_s.at[k],
        )

    own, rim = state(0), state(1)
    both = (own, rim)
    grp, sub = lax.axis_index("grp"), lax.axis_index("sub")
    devices = n_grp * n_sub
    me = grp * n_sub + sub

    def dev(by):
        other = lax.rem(me + by + devices, devices)
        return (lax.div(other, n_sub), lax.rem(other, n_sub))

    def in_group(by):
        return (grp, lax.rem(sub + by + n_sub, n_sub))

    def across(by):
        return (lax.rem(grp + by + n_grp, n_grp), sub)

    def has(by):
        return (me + by >= 0) & (me + by < devices)

    barrier = pltpu.get_barrier_semaphore()

    def greet(to):
        pl.semaphore_signal(barrier, inc=1, device_id=to, device_id_type=MESH)

    greeted = n_sub - 1 + n_grp - 1
    for by in (1, -1, 2, -2):
        pl.when(has(by))(functools.partial(greet, dev(by)))
        greeted = greeted + has(by).astype(I32)
    for by in range(1, n_sub):
        greet(in_group(by))
    for by in range(1, n_grp):
        greet(across(by))

    loads = [
        pltpu.make_async_copy(a, b, in_sem.at[i])
        for i, (a, b) in enumerate(
            ((mu, own.mu_v), (neigh, nb_v), (pot, own.u0_v), (rs, own.rs_v), (owner, own_v))
        )
    ]
    for copy in loads:
        copy.start()

    lane = lax.broadcasted_iota(I32, (BLK, LN), 1)
    xpos = lane & 15
    yrow = lane >> 4
    row = lax.broadcasted_iota(I32, (BLK, LN), 0)
    lane8 = lax.broadcasted_iota(I32, (8, LN), 1)
    row8 = lax.broadcasted_iota(I32, (8, LN), 0)
    x_first, x_last = xpos == 0, xpos == BE - 1
    x_face = x_first | x_last
    y_first, y_last = lane < BE, lane >= LN - BE
    even = (lane & 1) == 0
    zero = jnp.zeros((BLK, LN), F32)

    def turn(v, by):
        if isinstance(by, int):
            by = by % LN
            return v if by == 0 else pltpu.roll(v, by, 1)
        return pltpu.roll(v, by & (LN - 1), 1)

    def lower_y(v0, v1):
        a, b = turn(v0, BE), turn(v1, BE)
        return a, jnp.where(y_first, a, b)

    def upper_y(v0, v1):
        a, b = turn(v0, -BE), turn(v1, -BE)
        return jnp.where(y_last, b, a), b

    def remote(src, dst, a, b, to):
        return pltpu.make_async_remote_copy(
            src_ref=src, dst_ref=dst, send_sem=a, recv_sem=b, device_id=to, device_id_type=MESH
        )

    def faces_of(produce, faces_ref, plane):
        for zg in range(2):
            def body(i, carry, zg=zg):
                x0, x1, y2, y3 = carry
                v0, v1 = produce(zg, i)
                here = (xpos == 2 * i) | (xpos == ((2 * i + 15) & 15))
                x0 = jnp.where(here, turn(v0, 2 * i), x0)
                x1 = jnp.where(here, turn(v1, 2 * i), x1)
                line = yrow == i
                y2 = jnp.where(line, turn(v0, BE * i), y2)
                y3 = jnp.where(line, turn(v1, BE * i + BE), y3)
                return x0, x1, y2, y3

            x0, x1, y2, y3 = steps(8, body, (zero, zero, zero, zero))
            faces_ref[8 + 2 * zg] = x0
            faces_ref[9 + 2 * zg] = x1
            faces_ref[4 + zg] = y2
            faces_ref[6 + zg] = y3
        for h in range(2):
            faces_ref[h] = plane(0, h)
            faces_ref[2 + h] = plane(BE - 1, h)

    def sources(faces_ref, src_ref, is_rim=False):
        for k in range(12):
            if k < 8:
                v = faces_ref[SOURCE[k]]
            else:
                x = faces_ref[k]
                v = jnp.where(even, turn(x, -15), turn(x, 15))
            if is_rim:
                src_ref[k, 8:16, :] = v[0:8]
                src_ref[k, 32:40, :] = v[8:16]
            else:
                src_ref[k, 16:32, :] = v

    def send_faces(src_ref, slot):
        for m in range(6):
            pair = []
            for k in (2 * m, 2 * m + 1):
                edge = jnp.where(row8 < 4, src_ref[k, 16:24, :], src_ref[k, 24:32, :])
                way = route[GROUP[k]]
                d = jnp.zeros((8, LN), F32)
                for r in (4,) if k < 4 else range(1, 8):
                    d = jnp.where(way == r, pltpu.roll(edge, r, 0), d)
                pair.append(d)
                if slot:
                    keep[slot - 1, k] = d
            d0, d1 = pair
            send[slot, 0, m] = jnp.where(row8 < 4, d0, pltpu.roll(d1, 4, 0))
            send[slot, 1, m] = jnp.where(row8 < 4, pltpu.roll(d0, 4, 0), d1)
        start(face_copies(slot))

    def face_copies(slot):
        return [
            (
                remote(
                    send.at[slot, way],
                    recv.at[slot, way],
                    x_send.at[slot, way],
                    x_recv.at[slot, way],
                    dev(1 - 2 * way),
                ),
                1 - 2 * way,
            )
            for way in range(2)
        ]

    def local_ghosts(src_ref, ghost_ref):
        for k in range(12):
            r = rel_local[GROUP[k]]
            g = zero
            for by in (-4, 4) if k < 4 else range(-4, 5):
                g = jnp.where(r == by, src_ref[k, 16 + by : 32 + by, :], g)
            ghost_ref[k] = g

    def all_ghosts(src_ref, st):
        for k in range(12):
            r = st.rel[GROUP[k]]
            tops = (8, 32) if st is rim else (16, 24)
            for t in range(2):
                g = jnp.zeros((8, LN), F32)
                rt = r[8 * t : 8 * t + 8]
                for by in (-4, 4) if k < 4 else range(-4, 5):
                    g = jnp.where(rt == by, src_ref[k, tops[t] + by : tops[t] + by + 8, :], g)
                st.ghost[k, 8 * t : 8 * t + 8, :] = g

    def add_remote(slot, near_ref, ghost_ref):
        arrive(face_copies(slot))
        for m in range(6):
            lo, hi = recv[slot, 0, m], recv[slot, 1, m]
            lo1, hi0 = pltpu.roll(lo, 4, 0), pltpu.roll(hi, 4, 0)
            a, b = 2 * m, 2 * m + 1
            ghost_ref[a, 0:8, :] = near_ref[a, 0:8, :] + jnp.where(row8 < 4, lo, 0.0)
            ghost_ref[b, 0:8, :] = near_ref[b, 0:8, :] + jnp.where(row8 < 4, lo1, 0.0)
            ghost_ref[a, 8:16, :] = near_ref[a, 8:16, :] + jnp.where(row8 < 4, 0.0, hi0)
            ghost_ref[b, 8:16, :] = near_ref[b, 8:16, :] + jnp.where(row8 < 4, 0.0, hi)

    def rows_both_ways(src, dst, a, b):
        return [
            (remote(src(8), dst(0), a.at[0], b.at[0], dev(1)), 1),
            (remote(src(0), dst(8), a.at[1], b.at[1], dev(-1)), -1),
        ]

    def field_copies(k):
        ref = (mu_s, u0_s, rs_s, u0_s)[k]
        lanes = {1: pl.ds(0, 2048), 3: pl.ds(2048, 2048)}.get(k, pl.ds(0, 4096))
        return rows_both_ways(
            lambda r: ref.at[0, pl.ds(r, 8), lanes],
            lambda r: ref.at[1, pl.ds(r, 8), lanes],
            k_send.at[k],
            k_recv.at[k],
        )

    def ghost_copies(slot):
        return rows_both_ways(
            lambda r: near_local.at[slot, :, pl.ds(r, 8)],
            lambda r: near_far.at[slot, :, pl.ds(r, 8)],
            g_send.at[slot],
            g_recv.at[slot],
        )

    def coupling_copies():
        return rows_both_ways(
            lambda r: cface_s.at[0, :, pl.ds(r, 8)],
            lambda r: cface_s.at[1, :, pl.ds(r, 8)],
            c_send,
            c_recv,
        )

    def start(copies):
        for copy, by in copies:
            if by is None:
                copy.start()
            else:
                pl.when(has(by))(copy.start)

    def arrive(copies):
        for copy, by in copies:
            if by is None:
                copy.wait_recv()
            else:
                pl.when(has(-by))(copy.wait_recv)

    def finish(copies):
        for copy, by in copies:
            if by is None:
                copy.wait_send()
            else:
                pl.when(has(by))(copy.wait_send)

    def rim_ghosts(slot):
        arrive(ghost_copies(slot))
        for k in range(12):
            d = keep[slot, k]
            rim.ghost[k, 0:8, :] = near_far[slot, k, 0:8, :] + jnp.where(row8 < 4, 0.0, d)
            rim.ghost[k, 8:16, :] = near_far[slot, k, 8:16, :] + jnp.where(row8 < 4, d, 0.0)

    def spread_x(faces_ref, zg, i, h):
        return turn(faces_ref[8 + 2 * zg + h], LN - 2 * i)

    def spread_y(faces_ref, zg, i, h):
        return turn(faces_ref[(4, 6)[h] + zg], LN - BE * i - (0, BE)[h])

    first = BLK * me - MINE
    loads[1].wait()
    low = lax.div(first + LN, LN) - 1
    shift = first - low * LN
    tiles = nblk // LN

    def table(k):
        at = pl.multiple_of(lax.rem(k + tiles, tiles) * LN, LN)
        rows6 = nb_v[:, pl.ds(at, LN)]
        return jnp.concatenate([rows6, jnp.full((2, LN), -1, I32)], axis=0)

    back = LN - shift
    ta, tb = turn(table(low), back), turn(table(low + 1), back)
    ids = first + lane8
    nb = jnp.where(lane8 < back, ta, tb)
    nb = jnp.where((nb >= 0) & (ids >= 0) & (ids < nblk), nb - first, -1000).astype(F32)
    nbt = nb.T
    col[...] = nbt

    def columns(f, lo, n):
        return jnp.broadcast_to(col[lo : lo + n, f : f + 1], (n, LN))

    rowf = row.astype(F32)
    row8f = row8.astype(F32)
    rim_row = jnp.where(row < 8, rowf + (MINE - 8.0), rowf + (MINE + 8.0))
    far = jnp.zeros((BLK, LN), F32) + 99.0
    rels, routes, edges, full, rim_full, rim_edges = [], [], [], [], [], []
    for f in range(6):
        to = columns(f, MINE, 16)
        step = to - float(MINE) - rowf
        near = (to >= float(MINE)) & (to < MINE + 16.0)
        rels.append(jnp.where(near, step, far))
        full.append(step)
        edges.append(jnp.where(to < 0.0, 1.0, 0.0))
        before, after = columns(f, MINE - 8, 8), columns(f, MINE + 16, 8)
        to = jnp.concatenate([before, after], axis=0)
        rim_full.append(to - rim_row)
        rim_edges.append(jnp.where(to < 0.0, 1.0, 0.0))
        to8 = jnp.where(row8 < 4, after, before)
        j = jnp.where(row8 < 4, to8 - (MINE + 8.0), to8 - float(MINE))
        ok = jnp.where(row8 < 4, jnp.where(j >= 4.0, 1.0, 0.0), jnp.where(j >= 0.0, 1.0, 0.0))
        ok = ok * jnp.where(row8 < 4, jnp.where(j < 8.0, 1.0, 0.0), jnp.where(j < 4.0, 1.0, 0.0))
        r = row8f - j
        routes.append(jnp.where(ok > 0.5, jnp.where(r < 0.0, r + 8.0, r), 99.0))
    even8 = (lane8 & 1) == 0
    for g in range(4):
        rel_local[g], route[g] = rels[g], routes[g]
        own.rel[g], own.bnd[g] = full[g], edges[g]
        rim.rel[g], rim.bnd[g] = rim_full[g], rim_edges[g]
    rel_local[4] = jnp.where(even, rels[4], rels[5])
    route[4] = jnp.where(even8, routes[4], routes[5])
    own.rel[4] = jnp.where(even, full[4], full[5])
    own.bnd[4] = jnp.where(even, edges[4], edges[5])
    rim.rel[4] = jnp.where(even, rim_full[4], rim_full[5])
    rim.bnd[4] = jnp.where(even, rim_edges[4], rim_edges[5])
    for st, e in ((own, edges), (rim, rim_edges)):
        st.bx = jnp.where(x_first, e[4], jnp.where(x_last, e[5], 0.0))
        st.by = (jnp.where(y_first, e[2], 0.0), jnp.where(y_last, e[3], 0.0))

    def fill_way(way):
        for slot in range(N_X):
            for m in range(6):
                recv[slot, way, m] = jnp.zeros((8, LN), F32)

    def fill_blocks(by):
        at = MINE + 16 * by
        link_w[at : at + 16] = jnp.ones((16, LN), F32)
        share_w[at : at + 16] = jnp.zeros((16, LN), F32)

    for way in range(2):
        pl.when(jnp.logical_not(has(2 * way - 1)))(functools.partial(fill_way, way))
    for by in (1, -1, 2, -2):
        pl.when(jnp.logical_not(has(by)))(functools.partial(fill_blocks, by))

    def plane_of(ref):
        return lambda z, h: ref[:, z * 256 + h * LN : z * 256 + (h + 1) * LN]

    def from_input(ref, store=None):
        def produce(zg, i):
            at = pl.multiple_of((zg * 8 + i) * 256, 256)
            v0, v1 = ref[:, pl.ds(at, LN)], ref[:, pl.ds(at + LN, LN)]
            if store is not None:
                store[zg * 8 + i + 1, :, chunk(0)] = v0
                store[zg * 8 + i + 1, :, chunk(1)] = v1
            return v0, v1

        return produce

    loads[0].wait()
    faces_of(from_input(own.mu_v), own_mu, plane_of(own.mu_v))
    sources(own_mu, src_w)
    pl.semaphore_wait(barrier, greeted)
    send_faces(src_w, X_MU)
    loads[2].wait()
    faces_of(from_input(own.u0_v, own.u), own.faces, plane_of(own.u0_v))
    sources(own.faces, src_f)
    send_faces(src_f, X_U0)
    local_ghosts(src_f, near_local.at[0])
    loads[3].wait()
    start(field_copies(0))
    start(field_copies(2))
    start(field_copies(3))

    local_ghosts(src_w, mu_f)
    for st in both:
        for ref in (st.u, st.w):
            ref[0] = jnp.zeros((BLK, 256), F32)
            ref[BE + 1] = jnp.zeros((BLK, 256), F32)
        st.cz[0] = jnp.zeros((BLK, 256), F32)
        st.cz[BE] = jnp.zeros((BLK, 256), F32)

    def mean(a, b):
        return 2.0 * a * b / (a + b)

    def inner_couplings(st):
        def body(z):
            at = pl.multiple_of(z * 256, 256)
            m0, m1 = st.mu_v[:, pl.ds(at, LN)], st.mu_v[:, pl.ds(at + LN, LN)]
            y0, y1 = lower_y(m0, m1)
            st.cx[z, :, chunk(0)] = jnp.where(x_first, 0.0, mean(m0, turn(m0, 1)))
            st.cx[z, :, chunk(1)] = jnp.where(x_first, 0.0, mean(m1, turn(m1, 1)))
            st.cy[z, :, chunk(0)] = jnp.where(y_first, 0.0, mean(m0, y0))
            st.cy[z, :, chunk(1)] = mean(m1, y1)

        def across_z(z):
            at = pl.multiple_of(z * 256, 256)
            st.cz[z + 1] = mean(st.mu_v[:, pl.ds(at, 256)], st.mu_v[:, pl.ds(at + 256, 256)])

        steps(BE, body)
        steps(BE - 1, across_z)

    inner_couplings(own)

    def around(st, z):
        cx0, cx1 = st.cx[z, :, chunk(0)], st.cx[z, :, chunk(1)]
        cy0, cy1 = st.cy[z, :, chunk(0)], st.cy[z, :, chunk(1)]
        uy0, uy1 = upper_y(cy0, cy1)
        uy1 = jnp.where(y_last, 0.0, uy1)
        lo = (st.cz[z, :, chunk(0)], st.cz[z, :, chunk(1)])
        up = (st.cz[z + 1, :, chunk(0)], st.cz[z + 1, :, chunk(1)])
        return (
            (lo[0], up[0], cy0, uy0, cx0, turn(cx0, -1)),
            (lo[1], up[1], cy1, uy1, cx1, turn(cx1, -1)),
        )

    def beside(ref, z):
        v0, v1 = ref[z + 1, :, chunk(0)], ref[z + 1, :, chunk(1)]
        l0, l1 = lower_y(v0, v1)
        p0, p1 = upper_y(v0, v1)
        return (v0, v1), (
            (ref[z, :, chunk(0)], ref[z + 2, :, chunk(0)], l0, p0, turn(v0, 1), turn(v0, -1)),
            (ref[z, :, chunk(1)], ref[z + 2, :, chunk(1)], l1, p1, turn(v1, 1), turn(v1, -1)),
        )

    def first_terms(st):
        def body(z, acc):
            c = around(st, z)
            _, n = beside(st.u, z)
            for h in range(2):
                at = pl.multiple_of(z * 256 + h * LN, LN)
                r = st.rs_v[:, pl.ds(at, LN)]
                d = c[h][0]
                t = r + c[h][0] * n[h][0]
                for f in range(1, 6):
                    d = d + c[h][f]
                    t = t + c[h][f] * n[h][f]
                st.dint[z, :, chunk(h)] = d
                st.t0[z, :, chunk(h)] = t
                acc = acc + r
            return acc

        return steps(BE, body, zero)

    acc = first_terms(own)
    rsum[...] = jnp.broadcast_to(jnp.sum(acc, axis=1, keepdims=True), (BLK, LN))

    add_remote(X_MU, mu_f, own.ghost)
    for k in range(12):
        m = own_mu[k]
        g = jnp.where(own.bnd[GROUP[k]] > 0.5, m, own.ghost[k])
        own.cface[k] = mean(m, g)
    add_remote(X_U0, near_local.at[0], own.ghost)

    def add_first_z(st):
        for k in range(12):
            pface[k] = st.cface[k] * st.ghost[k]
        for h in range(2):
            st.dint[0, :, chunk(h)] += st.cface[h]
            st.dint[BE - 1, :, chunk(h)] += st.cface[2 + h]
            st.t0[0, :, chunk(h)] += pface[h]
            st.t0[BE - 1, :, chunk(h)] += pface[2 + h]

    y_face = (y_first, y_last)

    def sweep_first(st):
        def produce(zg, i):
            z = zg * 8 + i
            vs = []
            for h in range(2):
                d = st.dint[z, :, chunk(h)]
                t = st.t0[z, :, chunk(h)]
                d = d + jnp.where(x_face, spread_x(st.cface, zg, i, h), 0.0)
                d = d + jnp.where(y_face[h], spread_y(st.cface, zg, i, h), 0.0)
                t = t + jnp.where(x_face, spread_x(pface, zg, i, h), 0.0)
                t = t + jnp.where(y_face[h], spread_y(pface, zg, i, h), 0.0)
                q = RELAX_FINE / d
                st.inv[z, :, chunk(h)] = q
                v = (1.0 - RELAX_FINE) * st.u[z + 1, :, chunk(h)] + q * t
                st.u[z + 1, :, chunk(h)] = v
                vs.append(v)
            return vs

        return produce

    def each_plane(produce):
        for zg in range(2):
            steps(8, lambda i, zg=zg: (produce(zg, i), None)[1])

    def plane_u(ref):
        return lambda z, h: ref[z + 1, :, chunk(h)]

    add_first_z(own)
    faces_of(sweep_first(own), own.faces, plane_u(own.u))
    sources(own.faces, src_f)
    send_faces(src_f, X_U1)
    start(field_copies(1))
    start(ghost_copies(0))

    def coefficients(st):
        for h in range(2):
            st.gz[0, :, chunk(h)] = st.cface[h] * st.inv[0, :, chunk(h)]
            st.gz[1, :, chunk(h)] = st.cface[2 + h] * st.inv[BE - 1, :, chunk(h)]

        def produce(zg, i):
            z = zg * 8 + i
            c = around(st, z)
            for h in range(2):
                q = st.inv[z, :, chunk(h)]
                for f in range(6):
                    st.coef[f, z, :, chunk(h)] = c[h][f] * q
                at = pl.multiple_of(z * 256 + h * LN, LN)
                st.rhs[z, :, chunk(h)] = st.rs_v[:, pl.ds(at, LN)] * q
                fx = jnp.where(x_face, spread_x(st.cface, zg, i, h), 0.0) * q
                fy = jnp.where(y_face[h], spread_y(st.cface, zg, i, h), 0.0) * q
                st.gx[z, :, chunk(h)] = fx
                st.gy[z, :, chunk(h)] = fy
                st.w[z + 1, :, chunk(h)] = 1.0 - fx * st.bx - fy * st.by[h]

        each_plane(produce)
        for h in range(2):
            st.w[1, :, chunk(h)] -= st.gz[0, :, chunk(h)] * st.bnd[0]
            st.w[BE, :, chunk(h)] -= st.gz[1, :, chunk(h)] * st.bnd[1]

    def inner_sweep(st, ref, base_ref, with_rhs):
        def body(z):
            v, n = beside(ref, z)
            for h in range(2):
                b = (1.0 - RELAX_FINE) * v[h]
                if with_rhs:
                    b = b + st.rhs[z, :, chunk(h)]
                for f in range(6):
                    b = b + st.coef[f, z, :, chunk(h)] * n[h][f]
                base_ref[z, :, chunk(h)] = b

        steps(BE, body)

    def add_z(st, base_ref):
        for h in range(2):
            base_ref[0, :, chunk(h)] += st.gz[0, :, chunk(h)] * st.ghost[h]
            base_ref[BE - 1, :, chunk(h)] += st.gz[1, :, chunk(h)] * st.ghost[2 + h]

    def outer_sweep(st, base_ref, ref, fix=None):
        add_z(st, base_ref)

        def produce(zg, i):
            z = zg * 8 + i
            vs = []
            for h in range(2):
                v = base_ref[z, :, chunk(h)]
                if fix is not None:
                    v = v + fix
                v = v + st.gx[z, :, chunk(h)] * spread_x(st.ghost, zg, i, h)
                v = v + st.gy[z, :, chunk(h)] * spread_y(st.ghost, zg, i, h)
                ref[z + 1, :, chunk(h)] = v
                vs.append(v)
            return vs

        return produce

    local_ghosts(src_f, near_local.at[1])
    coefficients(own)
    inner_sweep(own, own.u, own.base, True)
    start(ghost_copies(1))
    start(coupling_copies())

    def face_sums(value):
        sums = []
        for f in range(4):
            s = value(2 * f) + value(2 * f + 1)
            sums.append(jnp.sum(s, axis=1, keepdims=True))
        s = value(8) + value(9) + value(10) + value(11)
        sums.append(jnp.sum(jnp.where(even, s, 0.0), axis=1, keepdims=True))
        sums.append(jnp.sum(jnp.where(even, 0.0, s), axis=1, keepdims=True))
        return sums

    links = face_sums(lambda k: own.cface[k])
    tile = zero
    link_total = links[0]
    for f in range(6):
        tile = jnp.where(lane == f, links[f], tile)
        if f:
            link_total = link_total + links[f]
    link_w[MINE : MINE + 16] = tile

    def spread_blocks(ref, a, b):
        mine = ref.at[pl.ds(MINE, 16)]
        return [
            (remote(mine, ref.at[pl.ds(MINE - 16 * by, 16)], a.at[i], b.at[i], dev(by)), by)
            for i, by in enumerate((1, -1, 2, -2))
        ]

    link_copies = spread_blocks(link_w, l_send, l_recv)
    start(link_copies)


    add_remote(X_U1, near_local.at[1], own.ghost)
    faces_of(outer_sweep(own, own.base, own.u), own.faces, plane_u(own.u))
    sums = face_sums(lambda k: own.cface[k] * own.faces[k])
    left = rsum[:, 0:1]
    group_left = left
    tile = zero
    for f in range(6):
        tile = jnp.where(lane == f, sums[f], tile)
        left = left - sums[f]
        group_left = group_left - sums[f] * edges[f][:, 0:1]
    share_w[MINE : MINE + 16] = jnp.where(lane == 6, left, tile)
    total[0] = jnp.where(
        lane8 < 64,
        jnp.sum(group_left, axis=0, keepdims=True),
        jnp.sum(link_total, axis=0, keepdims=True),
    )
    total_copies = [
        (remote(total.at[0], total.at[i], a_send.at[i], a_recv.at[i], in_group(i)), None)
        for i in range(1, n_sub)
    ]
    start(total_copies)

    sources(own.faces, src_f)
    send_faces(src_f, X_U2)
    share_copies = spread_blocks(share_w, s_send, s_recv)
    start(share_copies)
    local_ghosts(src_f, near_local.at[2])
    start(ghost_copies(2))

    inner_sweep(own, own.u, own.base, True)
    arrive(field_copies(0))
    inner_couplings(rim)
    arrive(field_copies(1) + field_copies(2) + field_copies(3))
    each_plane(from_input(rim.u0_v, rim.u))
    first_terms(rim)
    arrive(coupling_copies())
    rim_ghosts(0)
    add_first_z(rim)
    each_plane(sweep_first(rim))
    coefficients(rim)
    inner_sweep(rim, rim.u, rim.base, True)
    arrive(total_copies)
    part = total[0]
    for i in range(1, n_sub):
        part = part + total[i]
    group_total[0] = part
    group_copies = [
        (remote(group_total.at[0], group_total.at[i], b_send.at[i], b_recv.at[i], across(i)), None)
        for i in range(1, n_grp)
    ]
    start(group_copies)

    rim_ghosts(1)
    each_plane(outer_sweep(rim, rim.base, rim.u))
    inner_sweep(rim, rim.u, rim.base, True)

    arrive(link_copies)
    iw = lax.broadcasted_iota(I32, (WIN, WIN), 0)
    lw = lax.broadcasted_iota(I32, (WIN, WIN), 1)
    lwf = lw.astype(F32)
    diagonal = link_w[:, 0:1]
    for f in range(1, 6):
        diagonal = diagonal + link_w[:, f : f + 1]
    gain = RELAX_COARSE / diagonal
    ident = jnp.where(iw == lw, 1.0, 0.0)
    hot = [jnp.where(col[0:WIN, f : f + 1] == lwf, 1.0, 0.0) for f in range(6)]
    gmat = link_w[:, 0:1] * hot[0]
    for f in range(1, 6):
        gmat = gmat + link_w[:, f : f + 1] * hot[f]
    gmat = gmat * gain + (1.0 - RELAX_COARSE) * ident

    def product(a, b):
        return lax.dot_general(
            a,
            b,
            (((1,), (0,)), ((), ())),
            precision=lax.Precision.HIGHEST,
            preferred_element_type=F32,
        )

    ymat = ident + gmat
    ymat = ident + product(ymat, gmat)
    ymat = ident + product(ymat, gmat)
    scale = jnp.sum(ident * gain, axis=0, keepdims=True)

    def pick(m):
        return [m[MINE : MINE + 16], m[MINE - 8 : MINE], m[MINE + 16 : MINE + 24]]

    picks = jnp.concatenate(sum([pick(m) for m in [ident] + hot], []), axis=0)
    qmat[...] = product(picks, ymat) * scale

    def window_sweep(st, base_ref, win):
        add_z(st, base_ref)

        def produce(zg, i):
            z = zg * 8 + i
            for h in range(2):
                v = base_ref[z, :, chunk(h)]
                v = v + st.gx[z, :, chunk(h)] * spread_x(st.ghost, zg, i, h)
                v = v + st.gy[z, :, chunk(h)] * spread_y(st.ghost, zg, i, h)
                if st is rim:
                    win[2 * z + h, 0:8, :] = v[0:8]
                    win[2 * z + h, 24:32, :] = v[8:16]
                else:
                    win[2 * z + h, 8:24, :] = v

        each_plane(produce)

    def from_w(st):
        def produce(zg, i):
            z = zg * 8 + i
            return st.w[z + 1, :, chunk(0)], st.w[z + 1, :, chunk(1)]

        return produce

    for st in both:
        faces_of(from_w(st), st.wfaces, plane_u(st.w))
        sources(st.wfaces, src_w, st is rim)
        inner_sweep(st, st.w, st.base_w, False)
    for st in both:
        all_ghosts(src_w, st)
        window_sweep(st, st.base_w, window_w)

    arrive(share_copies)
    acc = ident * share_w[:, 6:7]
    iwf = iw.astype(F32)
    for f in range(6):
        acc = acc + jnp.where(nb[f : f + 1, 0:WIN] == iwf, share_w[:, (f ^ 1) : (f ^ 1) + 1], 0.0)
    source_row = jnp.sum(acc, axis=0, keepdims=True)
    fixed = jnp.sum(qmat[...] * source_row, axis=1, keepdims=True)
    for n, st in enumerate(both):
        fix = fixed[16 * n : 16 * n + 16]
        st.corr[0] = jnp.broadcast_to(fix, (BLK, LN))
        gains = []
        for f in range(6):
            at = 32 * (f + 1) + 16 * n
            gains.append(jnp.broadcast_to(fixed[at : at + 16] - fix, (BLK, LN)))
        for f in range(4):
            st.corr[1 + f] = gains[f]
        st.corr[5] = jnp.where(even, gains[4], gains[5])

    def third_sweep(st):
        for k in range(12):
            st.ghost[k] += st.corr[1 + GROUP[k]]
        produce = outer_sweep(st, st.base, st.u, st.corr[0])
        faces_of(produce, st.faces, plane_u(st.u))
        sources(st.faces, src_f, st is rim)

    add_remote(X_U2, near_local.at[2], own.ghost)
    third_sweep(own)
    inner_sweep(own, own.u, own.base, True)
    rim_ghosts(2)
    third_sweep(rim)
    inner_sweep(rim, rim.u, rim.base, True)
    for st in both:
        all_ghosts(src_f, st)

    for st in both:
        window_sweep(st, st.base, window)

    loads[4].wait()
    owners = own_v[...]
    starts = jnp.sum(jnp.where(owners < me, 1.0, 0.0)).astype(I32)
    count = jnp.sum(jnp.where(owners == me, 1.0, 0.0)).astype(I32)
    at = jnp.clip(starts - BLK * me + 8, 4, 12)
    row24 = lax.broadcasted_iota(I32, (CAP, LN), 0)
    live = row24 < count

    arrive(group_copies)
    part = group_total[0]
    for i in range(1, n_grp):
        part = part + group_total[i]
    level = part[0:1, 0:1] / part[0:1, 64:65]
    level = jnp.broadcast_to(level, (CAP, LN))

    out_copies = []
    for q in range(4):
        def emit(i, q=q):
            z = 4 * q + i
            for h in range(2):
                lanes = pl.ds(pl.multiple_of(z * 256 + h * LN, LN), LN)
                rows = pl.ds(at, CAP)
                v = window[2 * z + h, rows, :] + level * window_w[2 * z + h, rows, :]
                out_v[:, lanes] = jnp.where(live, v, 0.0)

        steps(4, emit)
        part = pl.ds(1024 * q, 1024)
        copy = pltpu.make_async_copy(out_v.at[:, part], out.at[:, part], o_sem.at[q])
        copy.start()
        out_copies.append(copy)

    for slot in range(N_X):
        finish(face_copies(slot))
    for slot in range(3):
        finish(ghost_copies(slot) + field_copies(slot))
    finish(field_copies(3))
    finish(coupling_copies() + link_copies + share_copies + total_copies + group_copies)
    for copy in out_copies:
        copy.wait()


def local(potential, right_side, permeability, new_owner, neighbours):
    n_grp, n_sub = lax.axis_size("grp"), lax.axis_size("sub")
    nblk = new_owner.shape[0]
    vmem = pltpu.VMEM
    plane = (BLK, 256)
    dma = pltpu.SemaphoreType.DMA
    faces = (12, BLK, LN)
    scratch = [
        vmem((2, BLK, 4096), F32),
        vmem((2, BLK, 4096), F32),
        vmem((2, BLK, 4096), F32),
        vmem((nblk // LN, LN), I32),
        vmem((6, nblk), I32),
        vmem((2, BE + 2, *plane), F32),
        vmem((2, BE + 2, *plane), F32),
        vmem((2, BE, *plane), F32),
        vmem((2, BE, *plane), F32),
        vmem((2, BE + 1, *plane), F32),
        vmem((2, BE, *plane), F32),
        vmem((2, BE, *plane), F32),
        vmem((2, BE, *plane), F32),
        vmem((2, 6, BE, *plane), F32),
        vmem((2, BE, *plane), F32),
        vmem((2, BE, *plane), F32),
        vmem((2, BE, *plane), F32),
        vmem((2, 2, *plane), F32),
        vmem((2, BE, *plane), F32),
        vmem((2, BE, *plane), F32),
        vmem((2, *faces), F32),
        vmem((2, *faces), F32),
        vmem((2, *faces), F32),
        vmem((2, *faces), F32),
        vmem((2, 5, BLK, LN), F32),
        vmem((2, 5, BLK, LN), F32),
        vmem((2, 6, BLK, LN), F32),
        vmem(faces, F32),
        vmem(faces, F32),
        vmem(faces, F32),
        vmem((12, 48, LN), F32),
        vmem((12, 48, LN), F32),
        vmem((3, *faces), F32),
        vmem((3, *faces), F32),
        vmem((3, 12, 8, LN), F32),
        vmem((5, BLK, LN), F32),
        vmem((5, 8, LN), F32),
        vmem((LN, 8), F32),
        vmem((224, WIN), F32),
        vmem((WIN, LN), F32),
        vmem((WIN, LN), F32),
        vmem((BLK, LN), F32),
        vmem((N_X, 2, 6, 8, LN), F32),
        vmem((N_X, 2, 6, 8, LN), F32),
        vmem((n_sub, 8, LN), F32),
        vmem((n_grp, 8, LN), F32),
        vmem((32, 40, LN), F32),
        vmem((32, 40, LN), F32),
        vmem((CAP, 4096), F32),
        dma((5,)),
        dma((4,)),
        dma((N_X, 2)),
        dma((N_X, 2)),
        dma((4,)),
        dma((4,)),
        dma((4,)),
        dma((4,)),
        dma((n_sub,)),
        dma((n_sub,)),
        dma((n_grp,)),
        dma((n_grp,)),
        dma((4, 2)),
        dma((4, 2)),
        dma((3, 2)),
        dma((3, 2)),
        dma((2,)),
        dma((2,)),
    ]
    return pl.pallas_call(
        functools.partial(kernel, n_grp, n_sub, nblk),
        out_shape=jax.ShapeDtypeStruct((CAP, 4096), F32),
        in_specs=[pl.BlockSpec(memory_space=pl.ANY)] * 5,
        out_specs=pl.BlockSpec(memory_space=pl.ANY),
        scratch_shapes=scratch,
        compiler_params=pltpu.CompilerParams(
            collective_id=0, has_side_effects=True, vmem_limit_bytes=60 * 1024 * 1024
        ),
        cost_estimate=pl.CostEstimate(
            flops=8_000_000, bytes_accessed=1_200_000, transcendentals=0
        ),
        name="cycle",
    )(potential, right_side, permeability, new_owner.reshape(nblk // LN, LN), neighbours)


def solution(mesh):
    in_specs = (P(("grp", "sub"), None), P(("grp", "sub"), None), P(("grp", "sub"), None), P(), P())
    out_specs = P(("grp", "sub"), None)
    return jax.shard_map(local, mesh=mesh, in_specs=in_specs, out_specs=out_specs, check_vma=False)
```
